512 devices in a mesh: attn: 32 (over y, z_hi), ffn: 16 (over x, z_lo, core).
Axes of the slice: x: 4, y: 8, z: 8 (z_hi: 4, z_lo: 2; z = z_hi * 2 + z_lo), core: 2. Of those that a mesh axis runs over, the one named last changes fastest.
Arguments:
- queries: bfloat16 [128, 64, 128], P('attn'), may hold values from -8 to 8
- new_keys: bfloat16 [128, 8, 128], P('attn'), may hold values from -8 to 8
- token_new_values: bfloat16 [128, 8, 128], P('attn'), may hold values from -6 to 6
- cache_keys: bfloat16 [128, 2048, 8, 128], P('attn', 'ffn'), may hold values from -8 to 8
- stored_cache_values: bfloat16 [128, 2048, 8, 128], P('attn', 'ffn'), may hold values from -6 to 6
- lengths: int32 [128], P('attn'), may hold values from 1 to 2048, 163840 in all
- residual_in: bfloat16 [128, 8192], P('ffn', 'attn'), may hold values from -6 to 6
- out_weight: bfloat16 [8192, 8192], P('ffn', 'attn'), may hold values from -0.0625 to 0.0625
- norm_gain: float32 [8192], P('attn'), may hold values from 0.1 to 1.9
- gate_weight: bfloat16 [8192, 14336], P('attn', 'ffn'), may hold values from -0.0625 to 0.0625
- up_weight: bfloat16 [8192, 14336], P('attn', 'ffn'), may hold values from -0.0625 to 0.0625
- down_weight: bfloat16 [14336, 8192], P('ffn', 'attn'), may hold values from -0.046875 to 0.046875
Outputs:
- attended: bfloat16 [128, 8192], P('attn', 'ffn')
- layer_out: bfloat16 [128, 8192], P('ffn', 'attn')
The draws below stay inside these ranges and needn't reach their ends.
Inputs may be any that keep to these rules, and one draw needn't show every extreme that they name: lengths[r] positions of row r are valid, from position 0; some row has all 2048.
All inputs are finite; a program needn't handle non-finite values. No bound on the sum of `lengths` on one device may be relied on, other than what follows from the above.
Results may differ from the reference program's by a relative error of at most 0.027.
Values may be sent and summed in bfloat16 or wider, within the bound.
A program may use at most 64 MiB of HBM per device.

```python
import math
import jax
import jax.numpy as jnp
import numpy as np
from jax import lax

D = 8192
QUERY_HEADS = 64
KEY_VALUE_HEADS = 8
HEAD_DIMENSION = 128
FF = 14336
CACHE_SLOTS = 2048
DECODE_ROWS = 128


def draw_queries(key, part):
    key = jax.random.fold_in(key, 11)
    value_rows = jnp.clip(jax.random.normal(key, (DECODE_ROWS, QUERY_HEADS, HEAD_DIMENSION), jnp.float32), -6.0, 6.0)
    return value_rows.astype(jnp.bfloat16)


def draw_new_keys(key, part):
    key = jax.random.fold_in(key, 12)
    value_rows = jnp.clip(jax.random.normal(key, (DECODE_ROWS, KEY_VALUE_HEADS, HEAD_DIMENSION), jnp.float32), -6.0, 6.0)
    return value_rows.astype(jnp.bfloat16)


def draw_cache_keys(key, part):
    key = jax.random.fold_in(key, 13)
    value_rows = jnp.clip(jax.random.normal(key, (DECODE_ROWS, CACHE_SLOTS, KEY_VALUE_HEADS, HEAD_DIMENSION), jnp.float32), -6.0, 6.0)
    return value_rows.astype(jnp.bfloat16)


def draw_residual_in(key, part):
    key = jax.random.fold_in(key, 14)
    ramp = jnp.arange(D, dtype=jnp.float32) / (D - 1)
    column_scale = 0.25 * 3.0 ** ramp
    value_rows = jnp.clip(jax.random.normal(key, (DECODE_ROWS, D), jnp.float32), -6.0, 6.0) * column_scale[None, :]
    return value_rows.astype(jnp.bfloat16)


def steps_of(stream_key, dims, shards, low, top_value):
    level = 1.0
    for axis_at, parts in shards:
        steps = jax.random.uniform(jax.random.fold_in(jax.random.fold_in(stream_key, 6), axis_at), (parts,), jnp.float32, low / len(shards), top_value / len(shards))
        level = level * jnp.repeat(jnp.exp(steps), dims[axis_at] // parts).reshape((-1,) + (1,) * (len(dims) - 1 - axis_at))
    return level


def length_profile(number_of, total, bound, slope):
    weights = [(1 << 20) // math.isqrt(grade ** slope) + 1 for grade in range(2, number_of + 1)]
    surplus, counts = total - bound - (number_of - 1), [1] * (number_of - 1)
    while surplus > 0:
        movable = [i for i in range(number_of - 1) if counts[i] < bound]
        whole, remaining = sum([weights[i] for i in movable]), surplus
        for i in movable:
            extra = min(bound - counts[i], max(1, remaining * weights[i] // whole), surplus)
            counts[i] = counts[i] + extra
            surplus = surplus - extra
    return np.array([bound] + counts)


def ragged(stream_key, number_of, total, reach, lean):
    if number_of == 2:
        one = jax.random.randint(stream_key, (), max(1, total - reach), min(reach, total - 1) + 1)
        return jnp.stack([one, total - one])
    sizes = jnp.asarray(length_profile(number_of, total, reach, lean), jnp.int32)
    pairs = (number_of - 1) // 2
    giver, taker = sizes[1:1 + 2 * pairs:2], sizes[2:2 + 2 * pairs:2]
    room = jnp.minimum(giver - 1, reach - taker)
    shifted = jax.random.randint(jax.random.fold_in(stream_key, 1), (pairs,), 0, 1 << 20) % (room + 1)
    sizes = sizes.at[1:1 + 2 * pairs:2].set(giver - shifted).at[2:2 + 2 * pairs:2].set(taker + shifted)
    return sizes[jax.random.permutation(jax.random.fold_in(stream_key, 2), number_of)]


def normal_values(stream_key, extent, deviation, most, pieces=(), held_as=jnp.bfloat16):
    loudness = steps_of(stream_key, extent, pieces, -0.22, 0.18) if pieces else 1.0
    drawn = jax.random.normal(stream_key, extent, jnp.float32) * deviation * loudness
    return jnp.minimum(jnp.maximum(drawn, -most), most).astype(held_as)


def setup_inputs(seed: int = 0) -> dict:
    key_of = jax.random.split(jax.random.key(seed), 13)
    return {
        "queries": draw_queries(jax.random.fold_in(key_of[12], 71), 0),
        "new_keys": draw_new_keys(jax.random.fold_in(key_of[12], 71), 0),
        "token_new_values": normal_values(key_of[2], (DECODE_ROWS, KEY_VALUE_HEADS, HEAD_DIMENSION), 1.0, 6.0, ((0, 32),)),
        "cache_keys": draw_cache_keys(jax.random.fold_in(key_of[12], 71), 0),
        "stored_cache_values": normal_values(key_of[4], (DECODE_ROWS, CACHE_SLOTS, KEY_VALUE_HEADS, HEAD_DIMENSION), 1.0, 6.0, ((0, 32), (1, 16))),
        "lengths": ragged(key_of[5], DECODE_ROWS, DECODE_ROWS * CACHE_SLOTS * 5 // 8, CACHE_SLOTS, 2).astype(jnp.int32),
        "residual_in": draw_residual_in(jax.random.fold_in(key_of[12], 71), 0),
        "out_weight": normal_values(key_of[7], (QUERY_HEADS * HEAD_DIMENSION, D), (QUERY_HEADS * HEAD_DIMENSION) ** -0.5, 0.0625, ((0, 16), (1, 32))),
        "norm_gain": jnp.clip(1.0 + 0.18 * jax.random.normal(key_of[8], (D,), jnp.float32), 0.1, 1.9),
        "gate_weight": normal_values(key_of[9], (D, FF), D ** -0.5, 0.0625, ((0, 32), (1, 16))),
        "up_weight": normal_values(key_of[10], (D, FF), D ** -0.5, 0.0625, ((0, 32), (1, 16))),
        "down_weight": normal_values(key_of[11], (FF, D), FF ** -0.5, 0.046875, ((0, 16), (1, 32))),
    }


def attend_row(items):
    query_vector, key_new, value_new, keys, value_rows, length = items
    scale = 1.0 / math.sqrt(HEAD_DIMENSION)
    grouped_heads = query_vector.astype(jnp.float32).reshape(KEY_VALUE_HEADS, QUERY_HEADS // KEY_VALUE_HEADS, HEAD_DIMENSION)
    scores = jnp.einsum('kgd,pkd->kgp', grouped_heads, keys.astype(jnp.float32)) * scale
    own_score = jnp.einsum('kgd,kd->kg', grouped_heads, key_new.astype(jnp.float32)) * scale
    valid = jnp.arange(CACHE_SLOTS) < length
    masked = jnp.where(valid[None, None, :], scores, -jnp.inf)
    highest = jnp.maximum(lax.optimization_barrier(jnp.max(masked, axis=-1)), own_score)
    raw = jnp.where(valid[None, None, :], jnp.exp(masked - highest[..., None]), 0.0)
    weights = lax.optimization_barrier(raw.astype(jnp.bfloat16)).astype(jnp.float32)
    own_weight = jnp.exp(own_score - highest)
    total = lax.optimization_barrier(jnp.sum(weights, axis=-1)) + own_weight
    summed = jnp.einsum('kgp,pkd->kgd', weights, value_rows.astype(jnp.float32))
    summed = summed + own_weight[..., None] * value_new.astype(jnp.float32)[:, None, :]
    return (summed / total[..., None]).reshape(QUERY_HEADS * HEAD_DIMENSION).astype(jnp.bfloat16)

def reference(queries, new_keys, token_new_values, cache_keys, stored_cache_values, lengths, residual_in, out_weight, norm_gain, gate_weight, up_weight, down_weight):
    attended = lax.map(attend_row, (queries, new_keys, token_new_values, cache_keys, stored_cache_values, lengths))
    projected = jnp.dot(attended, out_weight, preferred_element_type=jnp.float32)
    mixed = (residual_in.astype(jnp.float32) + projected).astype(jnp.bfloat16)
    wide = mixed.astype(jnp.float32)
    mean_square = lax.optimization_barrier(jnp.mean(wide * wide, axis=1))
    normed = (wide * lax.rsqrt(mean_square + 1e-05)[:, None] * norm_gain[None, :]).astype(jnp.bfloat16)
    gate = jnp.dot(normed, gate_weight, preferred_element_type=jnp.float32)
    upward = jnp.dot(normed, up_weight, preferred_element_type=jnp.float32)
    hidden = (jax.nn.silu(gate) * upward).astype(jnp.bfloat16)
    feed = jnp.dot(hidden, down_weight, preferred_element_type=jnp.float32)
    layer_out = (wide + feed).astype(jnp.bfloat16)
    return (attended, layer_out)
```

```python
import functools
import math

import jax
import jax.numpy as jnp
from jax import lax
from jax.experimental import pallas as pl
from jax.experimental.pallas import tpu as pltpu
from jax.sharding import PartitionSpec as P

MESH = pl.DeviceIdType.MESH
D = 8192
A = 32
F = 16
ROWS = 4
HEADS = 64
KV = 8
HD = 128
SPAN = 128
LOW = -1e30
FLOOR = -1e29
BF = jnp.bfloat16
F32 = jnp.float32


def dot(a, b):
    return jnp.dot(a, b, preferred_element_type=F32)


def dot_nt(a, b):
    return lax.dot_general(a, b, (((1,), (1,)), ((), ())), preferred_element_type=F32)


def kernel(
    q_ref, nk_ref, nv_ref, k_hbm, v_hbm, len_ref, res_ref, wo_hbm, gain_ref, wg_hbm, wu_hbm, wd_hbm,
    att_out, layer_out,
    k_s, v_s, wo_s, wg_s, wu_s, wd_s,
    snd_a, rcv_a, msg_b, rcv_b, snd_c, rcv_c, msg_e, rcv_e, snd_f, rcv_f, msg_g, rcv_g, snd_h, rcv_h,
    x_s, att_s, gath_s,
    load_sem, send_sem, recv_sem, recv_f_sem,
):
    a = lax.axis_index("attn")
    f = lax.axis_index("ffn")

    loads = [
        pltpu.make_async_copy(src, dst, load_sem.at[i])
        for i, (src, dst) in enumerate(
            [(k_hbm, k_s), (v_hbm, v_s), (wo_hbm, wo_s), (wg_hbm, wg_s), (wu_hbm, wu_s), (wd_hbm, wd_s)]
        )
    ]
    for load in loads:
        load.start()

    barrier = pltpu.get_barrier_semaphore()

    def greet_f(i, c):
        pl.semaphore_signal(barrier, inc=1, device_id=(a, lax.rem(f + i, F)), device_id_type=MESH)
        return c

    def greet_a(i, c):
        pl.semaphore_signal(barrier, inc=1, device_id=(lax.rem(a + i, A), f), device_id_type=MESH)
        return c

    lax.fori_loop(1, F, greet_f, 0)
    lax.fori_loop(1, A, greet_a, 0)

    def to_ffn(src_of, dst, phase):
        def body(i, c):
            to = lax.rem(f + i, F)
            pltpu.make_async_remote_copy(
                src_ref=src_of(to), dst_ref=dst.at[f], send_sem=send_sem.at[phase], recv_sem=recv_sem.at[phase],
                device_id=(a, to), device_id_type=MESH,
            ).start()
            return c

        lax.fori_loop(1, F, body, 0)

    def to_attn(src_of, dst, phase, sem_of):
        def body(i, c):
            to = lax.rem(a + i, A)
            pltpu.make_async_remote_copy(
                src_ref=src_of(to), dst_ref=dst.at[a], send_sem=send_sem.at[phase], recv_sem=sem_of,
                device_id=(to, f), device_id_type=MESH,
            ).start()
            return c

        lax.fori_loop(1, A, body, 0)

    def wait_all(buf, n, sem):
        view = buf.at[pl.ds(0, n - 1)]
        pltpu.make_async_copy(view, view, sem).wait()

    col = lax.broadcasted_iota(jnp.int32, (HEADS, SPAN * KV), 1)
    head = lax.broadcasted_iota(jnp.int32, (HEADS, SPAN * KV), 0)
    match = (col & 7) == (head >> 3)
    place = (col >> 3) + f * SPAN
    own_ok = jnp.logical_and(
        match[:, :HD], jnp.logical_and(col[:, :HD] < KV, jnp.full((HEADS, HD), f, jnp.int32) == 0)
    )
    low_lane = lax.broadcasted_iota(jnp.int32, (HEADS, HD), 1) < HD // 2
    scale = 1.0 / math.sqrt(HD)
    pad = jnp.zeros((HD - KV, HD), BF)
    loads[0].wait()
    loads[1].wait()
    for r in range(ROWS):
        q = q_ref[r]
        s = dot_nt(q, k_s[r]) * scale
        s = jnp.where(jnp.logical_and(match, place < len_ref[r]), s, LOW)
        own = dot_nt(q, jnp.concatenate([nk_ref[r], pad], axis=0)) * scale
        own = jnp.where(own_ok, own, LOW)
        m = jnp.maximum(jnp.max(s, axis=1, keepdims=True), jnp.max(own, axis=1, keepdims=True))
        m = jnp.maximum(m, FLOOR).astype(BF).astype(F32)
        p = jnp.exp(s - m).astype(BF)
        own_p = jnp.exp(own - m).astype(BF)
        total = jnp.sum(p.astype(F32), axis=1, keepdims=True) + jnp.sum(
            own_p.astype(F32), axis=1, keepdims=True
        )
        o = dot(p, v_s[r]) + dot(own_p, jnp.concatenate([nv_ref[r], pad], axis=0))
        stats = jnp.where(low_lane, jnp.broadcast_to(m, (HEADS, HD)), jnp.broadcast_to(total, (HEADS, HD)))
        x_s[pl.ds(r * HEADS, HEADS), :] = jnp.concatenate([o, stats], axis=1).astype(BF)
    n = ROWS * HEADS
    i = lax.broadcasted_iota(jnp.int32, (n, n), 0)
    j = lax.broadcasted_iota(jnp.int32, (n, n), 1)
    perm = (j == ((i >> 2) & 3) * HEADS + (i >> 4) * 4 + (i & 3)).astype(F32).astype(BF)
    snd_a[...] = dot(perm, x_s[...]).astype(BF).reshape(F, 16, 2 * HD)

    pl.semaphore_wait(barrier, A + F - 2)
    to_ffn(lambda to: snd_a.at[to], rcv_a, 0)
    rcv_a[f] = snd_a[f]
    wait_all(rcv_a, F, recv_sem.at[0])

    parts = rcv_a[...].astype(F32)
    low3 = lax.broadcasted_iota(jnp.int32, (F, 16, HD), 2) < HD // 2
    stats = parts[:, :, HD:]
    turned = pltpu.roll(stats.reshape(F * 16, HD), HD // 2, 1).reshape(F, 16, HD)
    m = jnp.where(low3, stats, turned)
    t = jnp.where(low3, turned, stats)
    e = jnp.exp(m - jnp.max(m, axis=0, keepdims=True))
    att = jnp.sum(parts[:, :, :HD] * e, axis=0) / jnp.sum(t * e, axis=0)
    msg_b[...] = att.astype(BF)
    to_attn(lambda to: msg_b, rcv_b, 1, recv_sem.at[1])
    rcv_b[a] = msg_b[...]
    att_s[...] = msg_b[...].astype(F32)
    for h in range(4):
        att_out[:, h * HD : (h + 1) * HD] = att_s[pl.ds(h, ROWS, stride=4), :].astype(BF)
    loads[2].wait()
    wait_all(rcv_b, A, recv_sem.at[1])

    gath_s[...] = rcv_b[...].astype(F32).reshape(A * 16, HD)
    lhs = jnp.concatenate([gath_s[pl.ds(h, A * ROWS, stride=4), :].astype(BF) for h in range(4)], axis=1)

    def halves(x):
        x = x.reshape(F, 8, 2 * HD)
        return jnp.concatenate([x[:, :, :HD], x[:, :, HD:]], axis=1)

    snd_c[...] = halves(dot(lhs, wo_s[...])).astype(BF)
    to_ffn(lambda to: snd_c.at[to], rcv_c, 2)
    rcv_c[f] = snd_c[f]
    res = res_ref[...].astype(F32)
    res = jnp.concatenate([res[:, :HD], res[:, HD:]], axis=0)
    wait_all(rcv_c, F, recv_sem.at[2])
    msg_e[...] = (res + jnp.sum(rcv_c[...].astype(F32), axis=0)).astype(BF)

    to_ffn(lambda to: msg_e, rcv_e, 3)
    rcv_e[f] = msg_e[...]
    loads[3].wait()
    loads[4].wait()
    wait_all(rcv_e, F, recv_sem.at[3])
    wide = rcv_e[...].astype(F32)
    left = wide[:, :8].reshape(F * 8, HD)
    right = wide[:, 8:].reshape(F * 8, HD)
    squares = jnp.sum(left * left + right * right, axis=1, keepdims=True)
    squares = jnp.broadcast_to(squares, (F * 8, HD)).reshape(F, 8, HD)
    gain = gain_ref[...]
    normed = jnp.concatenate([left * gain[:, :HD], right * gain[:, HD:]], axis=1).astype(BF)

    low_sub = lax.broadcasted_iota(jnp.int32, (F, 8, HD), 1) < 4
    turned = pltpu.roll(squares, 4, 1)
    for at, w, even_fill, odd_fill in ((0, wg_s, turned, squares), (32, wu_s, squares, turned)):
        y = dot(normed, w[...]).reshape(F, 8, 7 * HD)
        c = [y[:, :, k * HD : (k + 1) * HD] for k in range(7)]
        even = jnp.concatenate([c[0], c[1], c[2], jnp.where(low_sub, c[3], even_fill)], axis=1)
        odd = jnp.concatenate([c[4], c[5], c[6], jnp.where(low_sub, odd_fill, c[3])], axis=1)
        snd_f[:, 0, pl.ds(at, 32), :] = even.astype(BF)
        snd_f[:, 1, pl.ds(at, 32), :] = odd.astype(BF)
    to_attn(lambda to: snd_f.at[to // 2, lax.rem(to, 2)], rcv_f, 4, recv_f_sem.at[a])

    def add(i, acc):
        src = lax.rem(a + A - i, A)
        pltpu.make_async_copy(rcv_f.at[src], rcv_f.at[src], recv_f_sem.at[src]).wait()
        return acc + rcv_f[src].astype(F32)

    acc = lax.fori_loop(1, A, add, snd_f[a // 2, lax.rem(a, 2)].astype(F32))
    low8 = lax.broadcasted_iota(jnp.int32, (8, HD), 0) < 4
    is_even = jnp.full((8, HD), lax.rem(a, 2), jnp.int32) == 0
    x, y = acc[24:32], acc[56:64]
    square_even = jnp.where(low8, pltpu.roll(x, 4, 0), y)
    square_odd = jnp.where(low8, x, pltpu.roll(y, 4, 0))
    norm = lax.rsqrt(jnp.where(is_even, square_even, square_odd) / D + 1e-5)
    norm = jnp.concatenate([norm] * 4, axis=0)
    gate = acc[:32] * norm
    up = acc[32:] * norm
    msg_g[...] = (gate / (1.0 + jnp.exp(-gate)) * up).astype(BF)

    to_attn(lambda to: msg_g, rcv_g, 5, recv_sem.at[5])
    rcv_g[a] = msg_g[...]
    loads[5].wait()
    wait_all(rcv_g, A, recv_sem.at[5])
    hid = rcv_g[...].reshape(F, 2, 32, HD).astype(F32)
    even, odd = hid[:, 0], hid[:, 1]
    mid = jnp.where(low_sub, even[:, 24:32], odd[:, 24:32])
    cols = [even[:, :8], even[:, 8:16], even[:, 16:24], mid, odd[:, :8], odd[:, 8:16], odd[:, 16:24]]
    hidden = jnp.concatenate([c.reshape(F * 8, HD) for c in cols], axis=1).astype(BF)
    snd_h[...] = halves(dot(hidden, wd_s[...])).astype(BF)
    to_ffn(lambda to: snd_h.at[to], rcv_h, 6)
    rcv_h[f] = snd_h[f]
    wait_all(rcv_h, F, recv_sem.at[6])
    done = msg_e[...].astype(F32) + jnp.sum(rcv_h[...].astype(F32), axis=0)
    layer_out[...] = jnp.concatenate([done[:8], done[8:]], axis=1).astype(BF)

    wait_all(rcv_a, F, send_sem.at[0])
    wait_all(rcv_b, A, send_sem.at[1])
    wait_all(rcv_c, F, send_sem.at[2])
    wait_all(rcv_e, F, send_sem.at[3])
    wait_all(rcv_f, A, send_sem.at[4])
    wait_all(rcv_g, A, send_sem.at[5])
    wait_all(rcv_h, F, send_sem.at[6])


def on_device(q, nk, nv, ck, cv, lengths, res, wo, gain, wg, wu, wd):
    vmem = pl.BlockSpec(memory_space=pltpu.VMEM)
    hbm = pl.BlockSpec(memory_space=pl.ANY)
    smem = pl.BlockSpec(memory_space=pltpu.SMEM)
    V = pltpu.VMEM
    return pl.pallas_call(
        kernel,
        out_shape=(
            jax.ShapeDtypeStruct((ROWS, 4 * HD), BF),
            jax.ShapeDtypeStruct((8, 2 * HD), BF),
        ),
        in_specs=[vmem, vmem, vmem, hbm, hbm, smem, vmem, hbm, vmem, hbm, hbm, hbm],
        out_specs=(vmem, vmem),
        scratch_shapes=[
            V((ROWS, SPAN * KV, HD), BF),
            V((ROWS, SPAN * KV, HD), BF),
            V(wo.shape, BF),
            V(wg.shape, BF),
            V(wu.shape, BF),
            V(wd.shape, BF),
            V((F, 16, 2 * HD), BF),
            V((F, 16, 2 * HD), BF),
            V((16, HD), BF),
            V((A, 16, HD), BF),
            V((F, 16, HD), BF),
            V((F, 16, HD), BF),
            V((16, HD), BF),
            V((F, 16, HD), BF),
            V((F, 2, 64, HD), BF),
            V((A, 64, HD), BF),
            V((32, HD), BF),
            V((A, 32, HD), BF),
            V((F, 16, HD), BF),
            V((F, 16, HD), BF),
            V((ROWS * HEADS, 2 * HD), BF),
            V((16, HD), F32),
            V((A * 16, HD), F32),
            pltpu.SemaphoreType.DMA((6,)),
            pltpu.SemaphoreType.DMA((7,)),
            pltpu.SemaphoreType.DMA((7,)),
            pltpu.SemaphoreType.DMA((A,)),
        ],
        compiler_params=pltpu.CompilerParams(
            collective_id=0, has_side_effects=True, vmem_limit_bytes=40 * 1024 * 1024
        ),
    )(
        q, nk, nv,
        ck.reshape(ROWS, SPAN * KV, HD), cv.reshape(ROWS, SPAN * KV, HD),
        lengths, res, wo, gain.reshape(1, 2 * HD), wg, wu, wd,
    )


def solution(mesh):
    in_specs = (
        P("attn", None, None),
        P("attn", None, None),
        P("attn", None, None),
        P("attn", "ffn", None, None),
        P("attn", "ffn", None, None),
        P("attn"),
        P("ffn", "attn"),
        P("ffn", "attn"),
        P("attn"),
        P("attn", "ffn"),
        P("attn", "ffn"),
        P("ffn", "attn"),
    )
    return jax.shard_map(
        on_device, mesh=mesh, in_specs=in_specs, out_specs=(P("attn", "ffn"), P("ffn", "attn")), check_vma=False
    )
```

```python
import functools
import math

import jax
import jax.numpy as jnp
from jax import lax
from jax.experimental import pallas as pl
from jax.experimental.pallas import tpu as pltpu
from jax.sharding import PartitionSpec as P

MESH = pl.DeviceIdType.MESH
D = 8192
A = 32
F = 16
ROWS = 4
HEADS = 64
KV = 8
HD = 128
SPAN = 128
LOW = -1e30
FLOOR = -1e29
BF = jnp.bfloat16
F32 = jnp.float32
ATTN_SHIFTS = sorted(
    ((y, z) for y in range(8) for z in range(4) if y or z),
    key=lambda s: (-(min(s[0], 8 - s[0]) + 2 * min(s[1], 4 - s[1])), s),
)
FFN_SHIFTS = sorted(
    ((x, z, c) for x in range(4) for z in range(2) for c in range(2) if x or z or c),
    key=lambda s: (-(min(s[0], 4 - s[0]) + s[1] + s[2] / 2), s),
)


def attn_at(a, shift, sign=1):
    return ((((a >> 2) + sign * shift[0]) & 7) << 2) | ((a + sign * shift[1]) & 3)


def ffn_at(f, shift):
    return ((((f >> 2) + shift[0]) & 3) << 2) | ((f & 3) ^ (2 * shift[1] + shift[2]))


def dot(a, b):
    return jnp.dot(a, b, preferred_element_type=F32)


def dot_nt(a, b):
    return lax.dot_general(a, b, (((1,), (1,)), ((), ())), preferred_element_type=F32)


def kernel(
    q_ref, nk_ref, nv_ref, k_hbm, v_hbm, len_ref, res_ref, wo_hbm, gain_ref, wg_hbm, wu_hbm, wd_hbm,
    att_out, layer_out,
    k_s, v_s, wo_s, wg_s, wu_s, wd_s,
    snd_a, rcv_a, msg_b, rcv_b, snd_c, rcv_c, msg_e, rcv_e, snd_f, rcv_f, msg_g, rcv_g, snd_h, rcv_h,
    x_s, att_s, gath_s,
    load_sem, send_sem, recv_sem, recv_f_sem,
):
    a = lax.axis_index("attn")
    f = lax.axis_index("ffn")

    def load(src, dst, i):
        return pltpu.make_async_copy(src, dst, load_sem.at[i])

    caches = [(load(k_hbm.at[r], k_s.at[r], 2 * r), load(v_hbm.at[r], v_s.at[r], 2 * r + 1)) for r in range(ROWS)]
    loads = [
        load(src, dst, 2 * ROWS + i)
        for i, (src, dst) in enumerate([(wo_hbm, wo_s), (wg_hbm, wg_s), (wu_hbm, wu_s), (wd_hbm, wd_s)])
    ]
    for pair in caches:
        for copy in pair:
            copy.start()

    barrier = pltpu.get_barrier_semaphore()

    def greet_f(i, c):
        pl.semaphore_signal(barrier, inc=1, device_id=(a, lax.rem(f + i, F)), device_id_type=MESH)
        return c

    def greet_a(i, c):
        pl.semaphore_signal(barrier, inc=1, device_id=(lax.rem(a + i, A), f), device_id_type=MESH)
        return c

    lax.fori_loop(1, F, greet_f, 0)
    lax.fori_loop(1, A, greet_a, 0)

    def to_ffn(src_of, dst, phase):
        for shift in FFN_SHIFTS:
            to = ffn_at(f, shift)
            pltpu.make_async_remote_copy(
                src_ref=src_of(to), dst_ref=dst.at[f], send_sem=send_sem.at[phase], recv_sem=recv_sem.at[phase],
                device_id=(a, to), device_id_type=MESH,
            ).start()

    def to_attn(src_of, dst, phase, sem_of):
        for shift in ATTN_SHIFTS:
            to = attn_at(a, shift)
            pltpu.make_async_remote_copy(
                src_ref=src_of(to), dst_ref=dst.at[a], send_sem=send_sem.at[phase], recv_sem=sem_of,
                device_id=(to, f), device_id_type=MESH,
            ).start()

    def wait_all(buf, n, sem):
        view = buf.at[pl.ds(0, n - 1)]
        pltpu.make_async_copy(view, view, sem).wait()

    col = lax.broadcasted_iota(jnp.int32, (HEADS, SPAN * KV), 1)
    head = lax.broadcasted_iota(jnp.int32, (HEADS, SPAN * KV), 0)
    match = (col & 7) == (head >> 3)
    place = (col >> 3) + f * SPAN
    own_ok = jnp.logical_and(
        match[:, :HD], jnp.logical_and(col[:, :HD] < KV, jnp.full((HEADS, HD), f, jnp.int32) == 0)
    )
    low_lane = lax.broadcasted_iota(jnp.int32, (HEADS, HD), 1) < HD // 2
    scale = 1.0 / math.sqrt(HD)
    pad = jnp.zeros((HD - KV, HD), BF)
    for r in range(ROWS):
        q = q_ref[r]
        caches[r][0].wait()
        s = dot_nt(q, k_s[r]) * scale
        s = jnp.where(jnp.logical_and(match, place < len_ref[r]), s, LOW)
        own = dot_nt(q, jnp.concatenate([nk_ref[r], pad], axis=0)) * scale
        own = jnp.where(own_ok, own, LOW)
        m = jnp.maximum(jnp.max(s, axis=1, keepdims=True), jnp.max(own, axis=1, keepdims=True))
        m = jnp.maximum(m, FLOOR).astype(BF).astype(F32)
        p = jnp.exp(s - m).astype(BF)
        own_p = jnp.exp(own - m).astype(BF)
        total = jnp.sum(p.astype(F32), axis=1, keepdims=True) + jnp.sum(
            own_p.astype(F32), axis=1, keepdims=True
        )
        caches[r][1].wait()
        o = dot(p, v_s[r]) + dot(own_p, jnp.concatenate([nv_ref[r], pad], axis=0))
        stats = jnp.where(low_lane, jnp.broadcast_to(m, (HEADS, HD)), jnp.broadcast_to(total, (HEADS, HD)))
        x_s[pl.ds(r * HEADS, HEADS), :] = jnp.concatenate([o, stats], axis=1).astype(BF)
    for copy in loads:
        copy.start()
    n = ROWS * HEADS
    i = lax.broadcasted_iota(jnp.int32, (n, n), 0)
    j = lax.broadcasted_iota(jnp.int32, (n, n), 1)
    perm = (j == ((i >> 2) & 3) * HEADS + (i >> 4) * 4 + (i & 3)).astype(F32).astype(BF)
    snd_a[...] = dot(perm, x_s[...]).astype(BF).reshape(F, 16, 2 * HD)

    pl.semaphore_wait(barrier, A + F - 2)
    to_ffn(lambda to: snd_a.at[to], rcv_a, 0)
    rcv_a[f] = snd_a[f]
    wait_all(rcv_a, F, recv_sem.at[0])

    parts = rcv_a[...].astype(F32)
    low3 = lax.broadcasted_iota(jnp.int32, (F, 16, HD), 2) < HD // 2
    stats = parts[:, :, HD:]
    turned = pltpu.roll(stats.reshape(F * 16, HD), HD // 2, 1).reshape(F, 16, HD)
    m = jnp.where(low3, stats, turned)
    t = jnp.where(low3, turned, stats)
    e = jnp.exp(m - jnp.max(m, axis=0, keepdims=True))
    att = jnp.sum(parts[:, :, :HD] * e, axis=0) / jnp.sum(t * e, axis=0)
    msg_b[...] = att.astype(BF)
    to_attn(lambda to: msg_b, rcv_b, 1, recv_sem.at[1])
    rcv_b[a] = msg_b[...]
    att_s[...] = msg_b[...].astype(F32)
    for h in range(4):
        att_out[:, h * HD : (h + 1) * HD] = att_s[pl.ds(h, ROWS, stride=4), :].astype(BF)
    loads[0].wait()
    wait_all(rcv_b, A, recv_sem.at[1])

    gath_s[...] = rcv_b[...].astype(F32).reshape(A * 16, HD)
    lhs = jnp.concatenate([gath_s[pl.ds(h, A * ROWS, stride=4), :].astype(BF) for h in range(4)], axis=1)

    def halves(x):
        x = x.reshape(F, 8, 2 * HD)
        return jnp.concatenate([x[:, :, :HD], x[:, :, HD:]], axis=1)

    snd_c[...] = halves(dot(lhs, wo_s[...])).astype(BF)
    to_ffn(lambda to: snd_c.at[to], rcv_c, 2)
    rcv_c[f] = snd_c[f]
    res = res_ref[...].astype(F32)
    res = jnp.concatenate([res[:, :HD], res[:, HD:]], axis=0)
    wait_all(rcv_c, F, recv_sem.at[2])
    msg_e[...] = (res + jnp.sum(rcv_c[...].astype(F32), axis=0)).astype(BF)

    to_ffn(lambda to: msg_e, rcv_e, 3)
    rcv_e[f] = msg_e[...]
    loads[1].wait()
    loads[2].wait()
    wait_all(rcv_e, F, recv_sem.at[3])
    wide = rcv_e[...].astype(F32)
    left = wide[:, :8].reshape(F * 8, HD)
    right = wide[:, 8:].reshape(F * 8, HD)
    squares = jnp.sum(left * left + right * right, axis=1, keepdims=True)
    squares = jnp.broadcast_to(squares, (F * 8, HD)).reshape(F, 8, HD)
    gain = gain_ref[...]
    normed = jnp.concatenate([left * gain[:, :HD], right * gain[:, HD:]], axis=1).astype(BF)

    low_sub = lax.broadcasted_iota(jnp.int32, (F, 8, HD), 1) < 4
    turned = pltpu.roll(squares, 4, 1)
    for at, w, even_fill, odd_fill in ((0, wg_s, turned, squares), (32, wu_s, squares, turned)):
        y = dot(normed, w[...]).reshape(F, 8, 7 * HD)
        c = [y[:, :, k * HD : (k + 1) * HD] for k in range(7)]
        even = jnp.concatenate([c[0], c[1], c[2], jnp.where(low_sub, c[3], even_fill)], axis=1)
        odd = jnp.concatenate([c[4], c[5], c[6], jnp.where(low_sub, odd_fill, c[3])], axis=1)
        snd_f[:, 0, pl.ds(at, 32), :] = even.astype(BF)
        snd_f[:, 1, pl.ds(at, 32), :] = odd.astype(BF)
    to_attn(lambda to: snd_f.at[to // 2, lax.rem(to, 2)], rcv_f, 4, recv_f_sem.at[a])

    acc = snd_f[a // 2, lax.rem(a, 2)].astype(F32)
    for shift in reversed(ATTN_SHIFTS):
        src = attn_at(a, shift, -1)
        pltpu.make_async_copy(rcv_f.at[src], rcv_f.at[src], recv_f_sem.at[src]).wait()
        acc = acc + rcv_f[src].astype(F32)
    low8 = lax.broadcasted_iota(jnp.int32, (8, HD), 0) < 4
    is_even = jnp.full((8, HD), lax.rem(a, 2), jnp.int32) == 0
    x, y = acc[24:32], acc[56:64]
    square_even = jnp.where(low8, pltpu.roll(x, 4, 0), y)
    square_odd = jnp.where(low8, x, pltpu.roll(y, 4, 0))
    norm = lax.rsqrt(jnp.where(is_even, square_even, square_odd) / D + 1e-5)
    norm = jnp.concatenate([norm] * 4, axis=0)
    gate = acc[:32] * norm
    up = acc[32:] * norm
    msg_g[...] = (gate / (1.0 + jnp.exp(-gate)) * up).astype(BF)

    to_attn(lambda to: msg_g, rcv_g, 5, recv_sem.at[5])
    rcv_g[a] = msg_g[...]
    loads[3].wait()
    wait_all(rcv_g, A, recv_sem.at[5])
    hid = rcv_g[...].reshape(F, 2, 32, HD).astype(F32)
    even, odd = hid[:, 0], hid[:, 1]
    mid = jnp.where(low_sub, even[:, 24:32], odd[:, 24:32])
    cols = [even[:, :8], even[:, 8:16], even[:, 16:24], mid, odd[:, :8], odd[:, 8:16], odd[:, 16:24]]
    hidden = jnp.concatenate([c.reshape(F * 8, HD) for c in cols], axis=1).astype(BF)
    snd_h[...] = halves(dot(hidden, wd_s[...])).astype(BF)
    to_ffn(lambda to: snd_h.at[to], rcv_h, 6)
    rcv_h[f] = snd_h[f]
    wait_all(rcv_h, F, recv_sem.at[6])
    done = msg_e[...].astype(F32) + jnp.sum(rcv_h[...].astype(F32), axis=0)
    layer_out[...] = jnp.concatenate([done[:8], done[8:]], axis=1).astype(BF)

    wait_all(rcv_a, F, send_sem.at[0])
    wait_all(rcv_b, A, send_sem.at[1])
    wait_all(rcv_c, F, send_sem.at[2])
    wait_all(rcv_e, F, send_sem.at[3])
    wait_all(rcv_f, A, send_sem.at[4])
    wait_all(rcv_g, A, send_sem.at[5])
    wait_all(rcv_h, F, send_sem.at[6])


def on_device(q, nk, nv, ck, cv, lengths, res, wo, gain, wg, wu, wd):
    vmem = pl.BlockSpec(memory_space=pltpu.VMEM)
    hbm = pl.BlockSpec(memory_space=pl.ANY)
    smem = pl.BlockSpec(memory_space=pltpu.SMEM)
    V = pltpu.VMEM
    return pl.pallas_call(
        kernel,
        out_shape=(
            jax.ShapeDtypeStruct((ROWS, 4 * HD), BF),
            jax.ShapeDtypeStruct((8, 2 * HD), BF),
        ),
        in_specs=[vmem, vmem, vmem, hbm, hbm, smem, vmem, hbm, vmem, hbm, hbm, hbm],
        out_specs=(vmem, vmem),
        scratch_shapes=[
            V((ROWS, SPAN * KV, HD), BF),
            V((ROWS, SPAN * KV, HD), BF),
            V(wo.shape, BF),
            V(wg.shape, BF),
            V(wu.shape, BF),
            V(wd.shape, BF),
            V((F, 16, 2 * HD), BF),
            V((F, 16, 2 * HD), BF),
            V((16, HD), BF),
            V((A, 16, HD), BF),
            V((F, 16, HD), BF),
            V((F, 16, HD), BF),
            V((16, HD), BF),
            V((F, 16, HD), BF),
            V((F, 2, 64, HD), BF),
            V((A, 64, HD), BF),
            V((32, HD), BF),
            V((A, 32, HD), BF),
            V((F, 16, HD), BF),
            V((F, 16, HD), BF),
            V((ROWS * HEADS, 2 * HD), BF),
            V((16, HD), F32),
            V((A * 16, HD), F32),
            pltpu.SemaphoreType.DMA((2 * ROWS + 4,)),
            pltpu.SemaphoreType.DMA((7,)),
            pltpu.SemaphoreType.DMA((7,)),
            pltpu.SemaphoreType.DMA((A,)),
        ],
        compiler_params=pltpu.CompilerParams(
            collective_id=0, has_side_effects=True, vmem_limit_bytes=60 * 1024 * 1024
        ),
    )(
        q, nk, nv,
        ck.reshape(ROWS, SPAN * KV, HD), cv.reshape(ROWS, SPAN * KV, HD),
        lengths, res, wo, gain.reshape(1, 2 * HD), wg, wu, wd,
    )


def solution(mesh):
    in_specs = (
        P("attn", None, None),
        P("attn", None, None),
        P("attn", None, None),
        P("attn", "ffn", None, None),
        P("attn", "ffn", None, None),
        P("attn"),
        P("ffn", "attn"),
        P("ffn", "attn"),
        P("attn"),
        P("attn", "ffn"),
        P("attn", "ffn"),
        P("ffn", "attn"),
    )
    return jax.shard_map(
        on_device, mesh=mesh, in_specs=in_specs, out_specs=(P("attn", "ffn"), P("ffn", "attn")), check_vma=False
    )
```

```python
import functools
import math

import jax
import jax.numpy as jnp
from jax import lax
from jax.experimental import pallas as pl
from jax.experimental.pallas import tpu as pltpu
from jax.sharding import PartitionSpec as P

MESH = pl.DeviceIdType.MESH
D = 8192
A = 32
F = 16
ROWS = 4
HEADS = 64
KV = 8
HD = 128
SPAN = 128
LOW = -1e30
FLOOR = -1e29
BF = jnp.bfloat16
F32 = jnp.float32
ATTN_SHIFTS = sorted(
    ((y, z) for y in range(8) for z in range(4) if y or z),
    key=lambda s: (-(min(s[0], 8 - s[0]) + 2 * min(s[1], 4 - s[1])), s),
)
FFN_SHIFTS = sorted(
    ((x, z, c) for x in range(4) for z in range(2) for c in range(2) if x or z or c),
    key=lambda s: (-(min(s[0], 4 - s[0]) + s[1] + s[2] / 2), s),
)
COLUMN_SHIFTS = [s for s in ATTN_SHIFTS if s[0] % 2 == 0]
BLOCK_SHIFTS = sorted(
    ((x, z, c, w) for x in range(4) for z in range(2) for c in range(2) for w in range(3) if x or z or c or w),
    key=lambda s: (-(min(s[0], 4 - s[0]) + s[1] + s[2] / 2 + min(s[3], 1)), s),
)


def attn_at(a, shift, sign=1):
    return ((((a >> 2) + sign * shift[0]) & 7) << 2) | ((a + sign * shift[1]) & 3)


def ffn_at(f, shift):
    return ((((f >> 2) + shift[0]) & 3) << 2) | ((f & 3) ^ (2 * shift[1] + shift[2]))


def dot(a, b):
    return jnp.dot(a, b, preferred_element_type=F32)


def dot_nt(a, b):
    return lax.dot_general(a, b, (((1,), (1,)), ((), ())), preferred_element_type=F32)


def kernel(
    q_hbm, nk_hbm, nv_hbm, k_hbm, v_hbm, len_hbm, res_hbm, wo_hbm, gain_hbm, wg_hbm, wu_hbm, wd_hbm,
    att_out, layer_out,
    q_ref, nk_ref, nv_ref, len_ref, res_ref, gain_ref, k_s, v_s, wo_s, wg_s, wu_s, wd_s,
    snd_a, rcv_a, msg_b, rcv_b, snd_c, rcv_c, msg_e, rcv_e, snd_f, rcv_f, msg_g, rcv_g, snd_h, rcv_h,
    x_s, att_s, gath_s,
    load_sem, send_sem, recv_sem, recv_f_sem, give_send, give_recv,
):
    a = lax.axis_index("attn")
    f = lax.axis_index("ffn")
    odd = (a >> 2) & 1
    gate_with = a ^ 4
    up_with = ((((a >> 2) + 2 * odd - 1) & 7) << 2) | (a & 3)
    owners = (a, gate_with, up_with)
    group = ((a >> 3) << 2) | (a & 3)

    barrier = pltpu.get_barrier_semaphore()
    for shift in ATTN_SHIFTS:
        pl.semaphore_signal(barrier, inc=1, device_id=(attn_at(a, shift), f), device_id_type=MESH)
    for shift in BLOCK_SHIFTS:
        if shift[:3] != (0, 0, 0):
            peer = (owners[shift[3]], ffn_at(f, shift))
            pl.semaphore_signal(barrier, inc=1, device_id=peer, device_id_type=MESH)

    def load(src, dst, i):
        return pltpu.make_async_copy(src, dst, load_sem.at[i])

    small = [
        load(src, dst, 2 * ROWS + 6 + i)
        for i, (src, dst) in enumerate(
            [(q_hbm, q_ref), (nk_hbm, nk_ref), (nv_hbm, nv_ref), (len_hbm, len_ref), (res_hbm, res_ref), (gain_hbm, gain_ref.at[0])]
        )
    ]
    caches = [(load(k_hbm.at[r], k_s.at[r], 2 * r), load(v_hbm.at[r], v_s.at[r], 2 * r + 1)) for r in range(ROWS)]
    own_half = pl.ds(pl.multiple_of(odd * 4 * HD, HD), 3 * HD)
    their_half = pl.ds(pl.multiple_of((1 - odd) * 4 * HD, HD), 3 * HD)
    shared = pl.ds(3 * HD, HD)
    n0 = 2 * ROWS
    loads = [
        load(wo_hbm, wo_s, n0),
        load(wd_hbm, wd_s, n0 + 1),
        load(wg_hbm.at[:, own_half], wg_s.at[0, :, pl.ds(0, 3 * HD)], n0 + 2),
        load(wg_hbm.at[:, shared], wg_s.at[0, :, shared], n0 + 3),
        load(wu_hbm.at[:, own_half], wu_s.at[0, :, pl.ds(0, 3 * HD)], n0 + 4),
        load(wu_hbm.at[:, shared], wu_s.at[0, :, shared], n0 + 5),
    ]

    def give(src, dst, to, i):
        return pltpu.make_async_remote_copy(
            src_ref=src, dst_ref=dst, send_sem=give_send.at[i], recv_sem=give_recv.at[i],
            device_id=(to, f), device_id_type=MESH,
        )

    for copy in small:
        copy.start()
    for pair in caches:
        for copy in pair:
            copy.start()

    def to_ffn(src_of, dst, phase):
        for shift in FFN_SHIFTS:
            to = ffn_at(f, shift)
            pltpu.make_async_remote_copy(
                src_ref=src_of(to), dst_ref=dst.at[f], send_sem=send_sem.at[phase], recv_sem=recv_sem.at[phase],
                device_id=(a, to), device_id_type=MESH,
            ).start()

    def to_attn(src_of, dst, phase, sem_of):
        for shift in ATTN_SHIFTS:
            to = attn_at(a, shift)
            pltpu.make_async_remote_copy(
                src_ref=src_of(to), dst_ref=dst.at[a], send_sem=send_sem.at[phase], recv_sem=sem_of,
                device_id=(to, f), device_id_type=MESH,
            ).start()

    def wait_all(buf, n, sem):
        view = buf.at[pl.ds(0, n - 1)]
        pltpu.make_async_copy(view, view, sem).wait()

    col = lax.broadcasted_iota(jnp.int32, (HEADS, SPAN * KV), 1)
    head = lax.broadcasted_iota(jnp.int32, (HEADS, SPAN * KV), 0)
    match = (col & 7) == (head >> 3)
    place = (col >> 3) + f * SPAN
    own_ok = jnp.logical_and(
        match[:, :HD], jnp.logical_and(col[:, :HD] < KV, jnp.full((HEADS, HD), f, jnp.int32) == 0)
    )
    low_lane = lax.broadcasted_iota(jnp.int32, (HEADS, HD), 1) < HD // 2
    scale = 1.0 / math.sqrt(HD)
    pad = jnp.zeros((HD - KV, HD), BF)
    for copy in small:
        copy.wait()
    for r in range(ROWS):
        q = q_ref[r]
        caches[r][0].wait()
        s = dot_nt(q, k_s[r]) * scale
        s = jnp.where(jnp.logical_and(match, place < len_ref[r]), s, LOW)
        own = dot_nt(q, jnp.concatenate([nk_ref[r], pad], axis=0)) * scale
        own = jnp.where(own_ok, own, LOW)
        m = jnp.maximum(jnp.max(s, axis=1, keepdims=True), jnp.max(own, axis=1, keepdims=True))
        m = jnp.maximum(m, FLOOR).astype(BF).astype(F32)
        p = jnp.exp(s - m).astype(BF)
        own_p = jnp.exp(own - m).astype(BF)
        total = jnp.sum(p.astype(F32), axis=1, keepdims=True) + jnp.sum(
            own_p.astype(F32), axis=1, keepdims=True
        )
        caches[r][1].wait()
        o = dot(p, v_s[r]) + dot(own_p, jnp.concatenate([nv_ref[r], pad], axis=0))
        stats = jnp.where(low_lane, jnp.broadcast_to(m, (HEADS, HD)), jnp.broadcast_to(total, (HEADS, HD)))
        x_s[pl.ds(r * HEADS, HEADS), :] = jnp.concatenate([o, stats], axis=1).astype(BF)
    for copy in loads:
        copy.start()
    n = ROWS * HEADS
    i = lax.broadcasted_iota(jnp.int32, (n, n), 0)
    j = lax.broadcasted_iota(jnp.int32, (n, n), 1)
    perm = (j == ((i >> 2) & 3) * HEADS + (i >> 4) * 4 + (i & 3)).astype(F32).astype(BF)
    snd_a[...] = dot(perm, x_s[...]).astype(BF).reshape(F, 16, 2 * HD)

    pl.semaphore_wait(barrier, A - 1 + 3 * (F - 1))
    to_ffn(lambda to: snd_a.at[to], rcv_a, 0)
    gifts = [
        give(wg_hbm.at[:, their_half], wg_s.at[1, :, pl.ds(0, 3 * HD)], gate_with, 0),
        give(wu_hbm.at[:, their_half], wu_s.at[1, :, pl.ds(0, 3 * HD)], up_with, 1),
        give(wg_hbm.at[:, shared], wg_s.at[1, :, shared], gate_with, 2),
        give(wu_hbm.at[:, shared], wu_s.at[1, :, shared], up_with, 3),
        give(gain_ref.at[0], gain_ref.at[1], gate_with, 4),
        give(gain_ref.at[0], gain_ref.at[2], up_with, 5),
    ]
    rcv_a[f] = snd_a[f]
    wait_all(rcv_a, F, recv_sem.at[0])

    parts = rcv_a[...].astype(F32)
    low3 = lax.broadcasted_iota(jnp.int32, (F, 16, HD), 2) < HD // 2
    stats = parts[:, :, HD:]
    turned = pltpu.roll(stats.reshape(F * 16, HD), HD // 2, 1).reshape(F, 16, HD)
    m = jnp.where(low3, stats, turned)
    t = jnp.where(low3, turned, stats)
    e = jnp.exp(m - jnp.max(m, axis=0, keepdims=True))
    att = jnp.sum(parts[:, :, :HD] * e, axis=0) / jnp.sum(t * e, axis=0)
    msg_b[...] = att.astype(BF)
    to_attn(lambda to: msg_b, rcv_b, 1, recv_sem.at[1])
    for gift in gifts:
        gift.start()
    rcv_b[a] = msg_b[...]
    att_s[...] = msg_b[...].astype(F32)
    for h in range(4):
        att_out[:, h * HD : (h + 1) * HD] = att_s[pl.ds(h, ROWS, stride=4), :].astype(BF)
    loads[0].wait()
    wait_all(rcv_b, A, recv_sem.at[1])

    gath_s[...] = rcv_b[...].astype(F32).reshape(A * 16, HD)
    lhs = jnp.concatenate([gath_s[pl.ds(h, A * ROWS, stride=4), :].astype(BF) for h in range(4)], axis=1)

    def halves(x):
        x = x.reshape(F, 8, 2 * HD)
        return jnp.concatenate([x[:, :, :HD], x[:, :, HD:]], axis=1)

    snd_c[...] = halves(dot(lhs, wo_s[...])).astype(BF)
    to_ffn(lambda to: snd_c.at[to], rcv_c, 2)
    rcv_c[f] = snd_c[f]
    res = res_ref[...].astype(F32)
    res = jnp.concatenate([res[:, :HD], res[:, HD:]], axis=0)
    wait_all(rcv_c, F, recv_sem.at[2])
    msg_e[...] = (res + jnp.sum(rcv_c[...].astype(F32), axis=0)).astype(BF)

    for shift in BLOCK_SHIFTS:
        pltpu.make_async_remote_copy(
            src_ref=msg_e, dst_ref=rcv_e.at[shift[3] * F + f], send_sem=send_sem.at[3], recv_sem=recv_sem.at[3],
            device_id=(owners[shift[3]], ffn_at(f, shift)), device_id_type=MESH,
        ).start()
    rcv_e[f] = msg_e[...]
    for copy in loads[2:]:
        copy.wait()
    for gift in gifts:
        gift.wait_recv()
    wait_all(rcv_e, 3 * F, recv_sem.at[3])
    wide = rcv_e[...].astype(F32).reshape(3, F, 16, HD)
    squares = jnp.zeros((F * 8, 1), F32)
    normed = []
    for w in range(3):
        left = wide[w, :, :8].reshape(F * 8, HD)
        right = wide[w, :, 8:].reshape(F * 8, HD)
        if w < 2:
            squares = squares + jnp.sum(left * left + right * right, axis=1, keepdims=True)
        gain = gain_ref[w]
        normed.append(jnp.concatenate([left * gain[:, :HD], right * gain[:, HD:]], axis=1).astype(BF))
    squares = jnp.broadcast_to(squares, (F * 8, HD))

    gate = dot(normed[0], wg_s[0]) + dot(normed[1], wg_s[1])
    up = dot(normed[0], wu_s[0]) + dot(normed[2], wu_s[1])
    low = lax.broadcasted_iota(jnp.int32, (F * 8, HD), 1) < HD // 2
    is_odd = jnp.full((F * 8, HD), odd, jnp.int32) == 1
    gate3, up3 = gate[:, 3 * HD :], up[:, 3 * HD :]
    gate3 = jnp.where(is_odd, pltpu.roll(gate3, HD // 2, 1), gate3)
    up3 = jnp.where(is_odd, up3, pltpu.roll(up3, HD // 2, 1))
    tiles = [gate[:, k * HD : (k + 1) * HD] for k in range(3)] + [jnp.where(low, gate3, up3)]
    tiles += [up[:, k * HD : (k + 1) * HD] for k in range(3)] + [squares]
    snd_f[...] = jnp.concatenate([t.reshape(F, 8, HD) for t in tiles], axis=1).astype(BF)
    for shift in COLUMN_SHIFTS:
        to = attn_at(a, shift)
        pltpu.make_async_remote_copy(
            src_ref=snd_f.at[((to >> 3) << 2) | (to & 3)], dst_ref=rcv_f.at[group], send_sem=send_sem.at[4],
            recv_sem=recv_f_sem.at[group], device_id=(to, f), device_id_type=MESH,
        ).start()
    acc = snd_f[group].astype(F32)
    for shift in reversed(COLUMN_SHIFTS):
        src = attn_at(a, shift, -1)
        src = ((src >> 3) << 2) | (src & 3)
        pltpu.make_async_copy(rcv_f.at[src], rcv_f.at[src], recv_f_sem.at[src]).wait()
        acc = acc + rcv_f[src].astype(F32)
    norm = lax.rsqrt(acc[56:] / D + 1e-5)
    norm = jnp.concatenate([norm] * 4, axis=0)
    gate = acc[:32] * norm
    half = pltpu.roll(gate[24:], HD // 2, 1)
    up = jnp.concatenate([acc[32:56] * norm[:24], half], axis=0)
    hidden = gate / (1.0 + jnp.exp(-gate)) * up
    low = lax.broadcasted_iota(jnp.int32, (8, HD), 1) < HD // 2
    is_odd = jnp.full((8, HD), odd, jnp.int32) == 1
    half = jnp.where(is_odd, pltpu.roll(hidden[24:], HD // 2, 1), hidden[24:])
    msg_g[...] = jnp.concatenate([hidden[:24], half], axis=0).astype(BF)

    to_attn(lambda to: msg_g, rcv_g, 5, recv_sem.at[5])
    rcv_g[a] = msg_g[...]
    loads[1].wait()
    wait_all(rcv_g, A, recv_sem.at[5])
    hid = rcv_g[...].reshape(4, 2, 4, 32, HD).astype(F32)
    even = hid[:, 0].reshape(F, 32, HD)
    odds = hid[:, 1].reshape(F, 32, HD)
    low = lax.broadcasted_iota(jnp.int32, (F, 8, HD), 2) < HD // 2
    mid = jnp.where(low, even[:, 24:], odds[:, 24:])
    cols = [even[:, :8], even[:, 8:16], even[:, 16:24], mid, odds[:, :8], odds[:, 8:16], odds[:, 16:24]]
    hidden = jnp.concatenate([c.reshape(F * 8, HD) for c in cols], axis=1).astype(BF)
    snd_h[...] = halves(dot(hidden, wd_s[...])).astype(BF)
    to_ffn(lambda to: snd_h.at[to], rcv_h, 6)
    rcv_h[f] = snd_h[f]
    wait_all(rcv_h, F, recv_sem.at[6])
    done = msg_e[...].astype(F32) + jnp.sum(rcv_h[...].astype(F32), axis=0)
    layer_out[...] = jnp.concatenate([done[:8], done[8:]], axis=1).astype(BF)

    wait_all(rcv_a, F, send_sem.at[0])
    wait_all(rcv_b, A, send_sem.at[1])
    wait_all(rcv_c, F, send_sem.at[2])
    wait_all(rcv_e, 3 * F, send_sem.at[3])
    wait_all(rcv_f, F, send_sem.at[4])
    wait_all(rcv_g, A, send_sem.at[5])
    wait_all(rcv_h, F, send_sem.at[6])
    for gift in gifts:
        gift.wait_send()


def on_device(q, nk, nv, ck, cv, lengths, res, wo, gain, wg, wu, wd):
    vmem = pl.BlockSpec(memory_space=pltpu.VMEM)
    hbm = pl.BlockSpec(memory_space=pl.ANY)
    V = pltpu.VMEM
    return pl.pallas_call(
        kernel,
        out_shape=(
            jax.ShapeDtypeStruct((ROWS, 4 * HD), BF),
            jax.ShapeDtypeStruct((8, 2 * HD), BF),
        ),
        in_specs=[hbm] * 12,
        out_specs=(vmem, vmem),
        scratch_shapes=[
            V(q.shape, BF),
            V(nk.shape, BF),
            V(nv.shape, BF),
            pltpu.SMEM((ROWS,), jnp.int32),
            V(res.shape, BF),
            V((3, 1, 2 * HD), F32),
            V((ROWS, SPAN * KV, HD), BF),
            V((ROWS, SPAN * KV, HD), BF),
            V(wo.shape, BF),
            V((2, 2 * HD, 4 * HD), BF),
            V((2, 2 * HD, 4 * HD), BF),
            V(wd.shape, BF),
            V((F, 16, 2 * HD), BF),
            V((F, 16, 2 * HD), BF),
            V((16, HD), BF),
            V((A, 16, HD), BF),
            V((F, 16, HD), BF),
            V((F, 16, HD), BF),
            V((16, HD), BF),
            V((3 * F, 16, HD), BF),
            V((F, 64, HD), BF),
            V((F, 64, HD), BF),
            V((32, HD), BF),
            V((A, 32, HD), BF),
            V((F, 16, HD), BF),
            V((F, 16, HD), BF),
            V((ROWS * HEADS, 2 * HD), BF),
            V((16, HD), F32),
            V((A * 16, HD), F32),
            pltpu.SemaphoreType.DMA((2 * ROWS + 12,)),
            pltpu.SemaphoreType.DMA((7,)),
            pltpu.SemaphoreType.DMA((7,)),
            pltpu.SemaphoreType.DMA((F,)),
            pltpu.SemaphoreType.DMA((6,)),
            pltpu.SemaphoreType.DMA((6,)),
        ],
        compiler_params=pltpu.CompilerParams(
            collective_id=0, has_side_effects=True, vmem_limit_bytes=60 * 1024 * 1024
        ),
    )(
        q, nk, nv,
        ck.reshape(ROWS, SPAN * KV, HD), cv.reshape(ROWS, SPAN * KV, HD),
        lengths, res, wo, gain.reshape(1, 2 * HD), wg, wu, wd,
    )


def solution(mesh):
    in_specs = (
        P("attn", None, None),
        P("attn", None, None),
        P("attn", None, None),
        P("attn", "ffn", None, None),
        P("attn", "ffn", None, None),
        P("attn"),
        P("ffn", "attn"),
        P("ffn", "attn"),
        P("attn"),
        P("attn", "ffn"),
        P("attn", "ffn"),
        P("ffn", "attn"),
    )
    return jax.shard_map(
        on_device, mesh=mesh, in_specs=in_specs, out_specs=(P("attn", "ffn"), P("ffn", "attn")), check_vma=False
    )
```

```python
import functools
import math

import jax
import jax.numpy as jnp
from jax import lax
from jax.experimental import pallas as pl
from jax.experimental.pallas import tpu as pltpu
from jax.sharding import PartitionSpec as P

MESH = pl.DeviceIdType.MESH
D = 8192
A = 32
F = 16
ROWS = 4
HEADS = 64
KV = 8
HD = 128
SPAN = 128
LOW = -1e30
FLOOR = -1e29
BF = jnp.bfloat16
F32 = jnp.float32
ATTN_SHIFTS = sorted(
    ((y, z) for y in range(8) for z in range(4) if y or z),
    key=lambda s: (-(min(s[0], 8 - s[0]) + 2 * min(s[1], 4 - s[1])), s),
)
FFN_SHIFTS = sorted(
    ((x, z, c) for x in range(4) for z in range(2) for c in range(2) if x or z or c),
    key=lambda s: (-(min(s[0], 4 - s[0]) + s[1] + s[2] / 2), s),
)
COLUMN_SHIFTS = [s for s in ATTN_SHIFTS if s[0] % 2 == 0]
BLOCK_SHIFTS = sorted(
    ((x, c, w) for x in range(4) for c in range(2) for w in range(3) if x or c or w),
    key=lambda s: (-(min(s[0], 4 - s[0]) + s[1] / 2 + min(s[2], 1)), s),
)


def attn_at(a, shift, sign=1):
    return ((((a >> 2) + sign * shift[0]) & 7) << 2) | ((a + sign * shift[1]) & 3)


def ffn_at(f, shift):
    return ((((f >> 2) + shift[0]) & 3) << 2) | ((f & 3) ^ (2 * shift[1] + shift[2]))


def dot(a, b):
    return jnp.dot(a, b, preferred_element_type=F32)


def dot_nt(a, b):
    return lax.dot_general(a, b, (((1,), (1,)), ((), ())), preferred_element_type=F32)


def pair_of(f):
    return ((f >> 2) << 1) | (f & 1)


def in_pairs(x):
    return jnp.stack([x[(p >> 1) * 4 + z * 2 + (p & 1)] for p in range(F // 2) for z in range(2)], axis=0).reshape(
        (F // 2, 2) + x.shape[1:]
    )


def kernel(
    q_hbm, nk_hbm, nv_hbm, k_hbm, v_hbm, len_hbm, res_hbm, wo_hbm, gain_hbm, wg_hbm, wu_hbm, wd_hbm,
    fin,
    q_ref, nk_ref, nv_ref, len_ref, res_ref, gain_ref, k_s, v_s, wo_s, wg_s, wu_s, wd_s,
    snd_a, rcv_a, msg_b, rcv_b, snd_c, rcv_c, msg_e, rcv_e, snd_f, rcv_f, msg_g, rcv_g, snd_h, rcv_h,
    x_s, gath_s,
    load_sem, send_sem, recv_sem, recv_f_sem, give_send, give_recv, res_sem, res_s,
):
    a = lax.axis_index("attn")
    f = lax.axis_index("ffn")
    odd = (a >> 2) & 1
    gate_with = a ^ 4
    up_with = ((((a >> 2) + 2 * odd - 1) & 7) << 2) | (a & 3)
    owners = (a, gate_with, up_with)
    level = (f >> 1) & 1
    group = ((a >> 3) << 2) | (a & 3)

    barrier = pltpu.get_barrier_semaphore()
    for shift in FFN_SHIFTS:
        pl.semaphore_signal(barrier, inc=1, device_id=(a, ffn_at(f, shift)), device_id_type=MESH)
    for shift in ATTN_SHIFTS:
        pl.semaphore_signal(barrier, inc=1, device_id=(attn_at(a, shift), f), device_id_type=MESH)
    for x, c, w in BLOCK_SHIFTS:
        if w and (x or c):
            pl.semaphore_signal(barrier, inc=1, device_id=(owners[w], ffn_at(f, (x, 0, c))), device_id_type=MESH)

    def load(src, dst, i):
        return pltpu.make_async_copy(src, dst, load_sem.at[i])

    small = [
        load(src, dst, 2 * ROWS + 6 + i)
        for i, (src, dst) in enumerate(
            [(q_hbm, q_ref), (nk_hbm, nk_ref), (nv_hbm, nv_ref), (len_hbm, len_ref), (res_hbm, res_ref), (gain_hbm, gain_ref.at[0])]
        )
    ]
    caches = [(load(k_hbm.at[r], k_s.at[r], 2 * r), load(v_hbm.at[r], v_s.at[r], 2 * r + 1)) for r in range(ROWS)]
    own_half = pl.ds(pl.multiple_of(odd * 4 * HD, HD), 3 * HD)
    their_half = pl.ds(pl.multiple_of((1 - odd) * 4 * HD, HD), 3 * HD)
    shared = pl.ds(3 * HD, HD)
    n0 = 2 * ROWS
    loads = [
        load(wo_hbm, wo_s, n0),
        load(wd_hbm, wd_s, n0 + 1),
        load(wg_hbm.at[:, own_half], wg_s.at[0, :, pl.ds(0, 3 * HD)], n0 + 2),
        load(wg_hbm.at[:, shared], wg_s.at[0, :, shared], n0 + 3),
        load(wu_hbm.at[:, own_half], wu_s.at[0, :, pl.ds(0, 3 * HD)], n0 + 4),
        load(wu_hbm.at[:, shared], wu_s.at[0, :, shared], n0 + 5),
    ]

    def give(src, dst, to, i):
        return pltpu.make_async_remote_copy(
            src_ref=src, dst_ref=dst, send_sem=give_send.at[i], recv_sem=give_recv.at[i],
            device_id=(to, f), device_id_type=MESH,
        )

    for copy in small:
        copy.start()
    for pair in caches:
        for copy in pair:
            copy.start()

    def to_ffn(src_of, dst, phase):
        for shift in FFN_SHIFTS:
            to = ffn_at(f, shift)
            pltpu.make_async_remote_copy(
                src_ref=src_of(to), dst_ref=dst.at[f], send_sem=send_sem.at[phase], recv_sem=recv_sem.at[phase],
                device_id=(a, to), device_id_type=MESH,
            ).start()

    def to_attn(src_of, dst, phase, sem_of):
        for shift in ATTN_SHIFTS:
            to = attn_at(a, shift)
            pltpu.make_async_remote_copy(
                src_ref=src_of(to), dst_ref=dst.at[a], send_sem=send_sem.at[phase], recv_sem=sem_of,
                device_id=(to, f), device_id_type=MESH,
            ).start()

    def wait_all(buf, n, sem):
        view = buf.at[pl.ds(0, n - 1)]
        pltpu.make_async_copy(view, view, sem).wait()

    col = lax.broadcasted_iota(jnp.int32, (HEADS, SPAN * KV), 1)
    head = lax.broadcasted_iota(jnp.int32, (HEADS, SPAN * KV), 0)
    match = (col & 7) == (head >> 3)
    place = (col >> 3) + f * SPAN
    own_ok = jnp.logical_and(
        match[:, :HD], jnp.logical_and(col[:, :HD] < KV, jnp.full((HEADS, HD), f, jnp.int32) == 0)
    )
    low_lane = lax.broadcasted_iota(jnp.int32, (HEADS, HD), 1) < HD // 2
    scale = 1.0 / math.sqrt(HD)
    pad = jnp.zeros((HD - KV, HD), BF)
    for copy in small:
        copy.wait()
    for r in range(ROWS):
        q = q_ref[r]
        caches[r][0].wait()
        s = dot_nt(q, k_s[r]) * scale
        s = jnp.where(jnp.logical_and(match, place < len_ref[r]), s, LOW)
        own = dot_nt(q, jnp.concatenate([nk_ref[r], pad], axis=0)) * scale
        own = jnp.where(own_ok, own, LOW)
        m = jnp.maximum(jnp.max(s, axis=1, keepdims=True), jnp.max(own, axis=1, keepdims=True))
        m = jnp.maximum(m, FLOOR).astype(BF).astype(F32)
        p = jnp.exp(s - m).astype(BF)
        own_p = jnp.exp(own - m).astype(BF)
        total = jnp.sum(p.astype(F32), axis=1, keepdims=True) + jnp.sum(
            own_p.astype(F32), axis=1, keepdims=True
        )
        caches[r][1].wait()
        o = dot(p, v_s[r]) + dot(own_p, jnp.concatenate([nv_ref[r], pad], axis=0))
        stats = jnp.where(low_lane, jnp.broadcast_to(m, (HEADS, HD)), jnp.broadcast_to(total, (HEADS, HD)))
        x_s[pl.ds(r * HEADS, HEADS), :] = jnp.concatenate([o, stats], axis=1).astype(BF)
    for copy in loads:
        copy.start()
    n = ROWS * HEADS
    i = lax.broadcasted_iota(jnp.int32, (n, n), 0)
    j = lax.broadcasted_iota(jnp.int32, (n, n), 1)
    perm = (j == ((i >> 2) & 3) * HEADS + (i >> 4) * 4 + (i & 3)).astype(F32).astype(BF)
    snd_a[...] = dot(perm, x_s[...]).astype(BF).reshape(F, 16, 2 * HD)

    pl.semaphore_wait(barrier, A + F - 2 + 2 * (F // 2 - 1))
    res = res_ref[...].astype(F32)
    res_s[level] = jnp.concatenate([res[:, :HD], res[:, HD:]], axis=0).astype(BF)
    to_ffn(lambda to: snd_a.at[to], rcv_a, 0)
    res_gift = pltpu.make_async_remote_copy(
        src_ref=res_s.at[level], dst_ref=res_s.at[level], send_sem=res_sem.at[0], recv_sem=res_sem.at[1],
        device_id=(a, f ^ 2), device_id_type=MESH,
    )
    res_gift.start()
    gifts = [
        give(wg_hbm.at[:, their_half], wg_s.at[1, :, pl.ds(0, 3 * HD)], gate_with, 0),
        give(wu_hbm.at[:, their_half], wu_s.at[1, :, pl.ds(0, 3 * HD)], up_with, 1),
        give(wg_hbm.at[:, shared], wg_s.at[1, :, shared], gate_with, 2),
        give(wu_hbm.at[:, shared], wu_s.at[1, :, shared], up_with, 3),
        give(gain_ref.at[0], gain_ref.at[1], gate_with, 4),
        give(gain_ref.at[0], gain_ref.at[2], up_with, 5),
    ]
    rcv_a[f] = snd_a[f]
    wait_all(rcv_a, F, recv_sem.at[0])

    parts = rcv_a[...].astype(F32)
    low3 = lax.broadcasted_iota(jnp.int32, (F, 16, HD), 2) < HD // 2
    stats = parts[:, :, HD:]
    turned = pltpu.roll(stats.reshape(F * 16, HD), HD // 2, 1).reshape(F, 16, HD)
    m = jnp.where(low3, stats, turned)
    t = jnp.where(low3, turned, stats)
    e = jnp.exp(m - jnp.max(m, axis=0, keepdims=True))
    att = jnp.sum(parts[:, :, :HD] * e, axis=0) / jnp.sum(t * e, axis=0)
    msg_b[...] = att.astype(BF)
    to_attn(lambda to: msg_b, rcv_b, 1, recv_sem.at[1])
    for gift in gifts:
        gift.start()
    rcv_b[a] = msg_b[...]
    fin[:16] = msg_b[...].astype(F32)
    loads[0].wait()
    wait_all(rcv_b, A, recv_sem.at[1])

    gath_s[...] = rcv_b[...].astype(F32).reshape(A * 16, HD)
    lhs = jnp.concatenate([gath_s[pl.ds(h, A * ROWS, stride=4), :].astype(BF) for h in range(4)], axis=1)

    def halves(x):
        x = x.reshape(F, 8, 2 * HD)
        return jnp.concatenate([x[:, :, :HD], x[:, :, HD:]], axis=1)

    snd_c[...] = in_pairs(halves(dot(lhs, wo_s[...]))).astype(BF)
    for shift in FFN_SHIFTS:
        to = ffn_at(f, shift)
        pltpu.make_async_remote_copy(
            src_ref=snd_c.at[pair_of(to)], dst_ref=rcv_c.at[f], send_sem=send_sem.at[2], recv_sem=recv_sem.at[2],
            device_id=(a, to), device_id_type=MESH,
        ).start()
    rcv_c[f] = snd_c[pair_of(f)]
    res_gift.wait_recv()
    wait_all(rcv_c, F, recv_sem.at[2])
    msg_e[...] = (res_s[...].astype(F32) + jnp.sum(rcv_c[...].astype(F32), axis=0)).astype(BF)

    for x, c, w in BLOCK_SHIFTS:
        pltpu.make_async_remote_copy(
            src_ref=msg_e, dst_ref=rcv_e.at[w * (F // 2) + pair_of(f)], send_sem=send_sem.at[3], recv_sem=recv_sem.at[3],
            device_id=(owners[w], ffn_at(f, (x, 0, c))), device_id_type=MESH,
        ).start()
    rcv_e[pair_of(f)] = msg_e[...]
    for copy in loads[2:]:
        copy.wait()
    for gift in gifts:
        gift.wait_recv()
    wait_all(rcv_e, 3 * F // 2, recv_sem.at[3])
    wide = rcv_e[...].astype(F32).reshape(3, F, 16, HD)
    squares = jnp.zeros((F * 8, 1), F32)
    normed = []
    for w in range(3):
        left = wide[w, :, :8].reshape(F * 8, HD)
        right = wide[w, :, 8:].reshape(F * 8, HD)
        if w < 2:
            squares = squares + jnp.sum(left * left + right * right, axis=1, keepdims=True)
        gain = gain_ref[w]
        normed.append(jnp.concatenate([left * gain[:, :HD], right * gain[:, HD:]], axis=1).astype(BF))
    squares = jnp.broadcast_to(squares, (F * 8, HD))

    gate = dot(normed[0], wg_s[0]) + dot(normed[1], wg_s[1])
    up = dot(normed[0], wu_s[0]) + dot(normed[2], wu_s[1])
    low = lax.broadcasted_iota(jnp.int32, (F * 8, HD), 1) < HD // 2
    is_odd = jnp.full((F * 8, HD), odd, jnp.int32) == 1
    gate3, up3 = gate[:, 3 * HD :], up[:, 3 * HD :]
    gate3 = jnp.where(is_odd, pltpu.roll(gate3, HD // 2, 1), gate3)
    up3 = jnp.where(is_odd, up3, pltpu.roll(up3, HD // 2, 1))
    tiles = [gate[:, k * HD : (k + 1) * HD] for k in range(3)] + [jnp.where(low, gate3, up3)]
    tiles += [up[:, k * HD : (k + 1) * HD] for k in range(3)] + [squares]
    snd_f[...] = jnp.concatenate([t.reshape(F, 8, HD) for t in tiles], axis=1).astype(BF)
    for shift in COLUMN_SHIFTS:
        to = attn_at(a, shift)
        pltpu.make_async_remote_copy(
            src_ref=snd_f.at[((to >> 3) << 2) | (to & 3)], dst_ref=rcv_f.at[group], send_sem=send_sem.at[4],
            recv_sem=recv_f_sem.at[group], device_id=(to, f), device_id_type=MESH,
        ).start()
    acc = snd_f[group].astype(F32)
    for shift in reversed(COLUMN_SHIFTS):
        src = attn_at(a, shift, -1)
        src = ((src >> 3) << 2) | (src & 3)
        pltpu.make_async_copy(rcv_f.at[src], rcv_f.at[src], recv_f_sem.at[src]).wait()
        acc = acc + rcv_f[src].astype(F32)
    norm = lax.rsqrt(acc[56:] / D + 1e-5)
    norm = jnp.concatenate([norm] * 4, axis=0)
    gate = acc[:32] * norm
    half = pltpu.roll(gate[24:], HD // 2, 1)
    up = jnp.concatenate([acc[32:56] * norm[:24], half], axis=0)
    hidden = gate / (1.0 + jnp.exp(-gate)) * up
    low = lax.broadcasted_iota(jnp.int32, (8, HD), 1) < HD // 2
    is_odd = jnp.full((8, HD), odd, jnp.int32) == 1
    half = jnp.where(is_odd, pltpu.roll(hidden[24:], HD // 2, 1), hidden[24:])
    msg_g[...] = jnp.concatenate([hidden[:24], half], axis=0).astype(BF)

    to_attn(lambda to: msg_g, rcv_g, 5, recv_sem.at[5])
    rcv_g[a] = msg_g[...]
    loads[1].wait()
    wait_all(rcv_g, A, recv_sem.at[5])
    hid = rcv_g[...].reshape(4, 2, 4, 32, HD).astype(F32)
    even = hid[:, 0].reshape(F, 32, HD)
    odds = hid[:, 1].reshape(F, 32, HD)
    low = lax.broadcasted_iota(jnp.int32, (F, 8, HD), 2) < HD // 2
    mid = jnp.where(low, even[:, 24:], odds[:, 24:])
    cols = [even[:, :8], even[:, 8:16], even[:, 16:24], mid, odds[:, :8], odds[:, 8:16], odds[:, 16:24]]
    hidden = jnp.concatenate([c.reshape(F * 8, HD) for c in cols], axis=1).astype(BF)
    snd_h[...] = halves(dot(hidden, wd_s[...])).astype(BF)
    to_ffn(lambda to: snd_h.at[pair_of(to) * 2 + ((to >> 1) & 1)], rcv_h, 6)
    rcv_h[f] = snd_h[pair_of(f) * 2 + level]
    wait_all(rcv_h, F, recv_sem.at[6])
    done = msg_e[level].astype(F32) + jnp.sum(rcv_h[...].astype(F32), axis=0)
    fin[16:] = done

    wait_all(rcv_a, F, send_sem.at[0])
    wait_all(rcv_b, A, send_sem.at[1])
    wait_all(rcv_c, F, send_sem.at[2])
    wait_all(rcv_e, 3 * F // 2, send_sem.at[3])
    res_gift.wait_send()
    wait_all(rcv_f, F, send_sem.at[4])
    wait_all(rcv_g, A, send_sem.at[5])
    wait_all(rcv_h, F, send_sem.at[6])
    for gift in gifts:
        gift.wait_send()


def finish(fin, att_out, layer_out):
    for h in range(4):
        att_out[:, h * HD : (h + 1) * HD] = fin[pl.ds(h, ROWS, stride=4), :].astype(BF)
    layer_out[...] = jnp.concatenate([fin[16:24], fin[24:]], axis=1).astype(BF)


def on_device(q, nk, nv, ck, cv, lengths, res, wo, gain, wg, wu, wd):
    vmem = pl.BlockSpec(memory_space=pltpu.VMEM)
    hbm = pl.BlockSpec(memory_space=pl.ANY)
    V = pltpu.VMEM
    fin = pl.pallas_call(
        kernel,
        out_shape=jax.ShapeDtypeStruct((32, HD), F32),
        in_specs=[hbm] * 12,
        out_specs=vmem,
        scratch_shapes=[
            V(q.shape, BF),
            V(nk.shape, BF),
            V(nv.shape, BF),
            pltpu.SMEM((ROWS,), jnp.int32),
            V(res.shape, BF),
            V((3, 1, 2 * HD), F32),
            V((ROWS, SPAN * KV, HD), BF),
            V((ROWS, SPAN * KV, HD), BF),
            V(wo.shape, BF),
            V((2, 2 * HD, 4 * HD), BF),
            V((2, 2 * HD, 4 * HD), BF),
            V(wd.shape, BF),
            V((F, 16, 2 * HD), BF),
            V((F, 16, 2 * HD), BF),
            V((16, HD), BF),
            V((A, 16, HD), BF),
            V((F // 2, 2, 16, HD), BF),
            V((F, 2, 16, HD), BF),
            V((2, 16, HD), BF),
            V((3 * F // 2, 2, 16, HD), BF),
            V((F, 64, HD), BF),
            V((F, 64, HD), BF),
            V((32, HD), BF),
            V((A, 32, HD), BF),
            V((F, 16, HD), BF),
            V((F, 16, HD), BF),
            V((ROWS * HEADS, 2 * HD), BF),
            V((A * 16, HD), F32),
            pltpu.SemaphoreType.DMA((2 * ROWS + 12,)),
            pltpu.SemaphoreType.DMA((7,)),
            pltpu.SemaphoreType.DMA((7,)),
            pltpu.SemaphoreType.DMA((F,)),
            pltpu.SemaphoreType.DMA((6,)),
            pltpu.SemaphoreType.DMA((6,)),
            pltpu.SemaphoreType.DMA((2,)),
            V((2, 16, HD), BF),
        ],
        compiler_params=pltpu.CompilerParams(
            collective_id=0, has_side_effects=True, vmem_limit_bytes=60 * 1024 * 1024
        ),
    )(
        q, nk, nv,
        ck.reshape(ROWS, SPAN * KV, HD), cv.reshape(ROWS, SPAN * KV, HD),
        lengths, res, wo, gain.reshape(1, 2 * HD), wg, wu, wd,
    )
    return pl.pallas_call(
        finish,
        out_shape=(jax.ShapeDtypeStruct((ROWS, 4 * HD), BF), jax.ShapeDtypeStruct((8, 2 * HD), BF)),
        in_specs=[vmem],
        out_specs=(vmem, vmem),
    )(fin)


def solution(mesh):
    in_specs = (
        P("attn", None, None),
        P("attn", None, None),
        P("attn", None, None),
        P("attn", "ffn", None, None),
        P("attn", "ffn", None, None),
        P("attn"),
        P("ffn", "attn"),
        P("ffn", "attn"),
        P("attn"),
        P("attn", "ffn"),
        P("attn", "ffn"),
        P("ffn", "attn"),
    )
    return jax.shard_map(
        on_device, mesh=mesh, in_specs=in_specs, out_specs=(P("attn", "ffn"), P("ffn", "attn")), check_vma=False
    )
```

```python
import functools
import math

import jax
import jax.numpy as jnp
from jax import lax
from jax.experimental import pallas as pl
from jax.experimental.pallas import tpu as pltpu
from jax.sharding import PartitionSpec as P

MESH = pl.DeviceIdType.MESH
D = 8192
A = 32
F = 16
ROWS = 4
HEADS = 64
KV = 8
HD = 128
SPAN = 128
LOW = -1e30
FLOOR = -1e29
BF = jnp.bfloat16
F32 = jnp.float32
ATTN_SHIFTS = sorted(
    ((y, z) for y in range(8) for z in range(4) if y or z),
    key=lambda s: (-(min(s[0], 8 - s[0]) + 2 * min(s[1], 4 - s[1])), s),
)
FFN_SHIFTS = sorted(
    ((x, z, c) for x in range(4) for z in range(2) for c in range(2) if x or z or c),
    key=lambda s: (-(min(s[0], 4 - s[0]) + s[1] + s[2] / 2), s),
)
COLUMN_SHIFTS = [s for s in ATTN_SHIFTS if s[0] % 2 == 0]
BLOCK_SHIFTS = sorted(
    ((x, c, w) for x in range(4) for c in range(2) for w in range(3) if x or c or w),
    key=lambda s: (-(min(s[0], 4 - s[0]) + s[1] / 2 + min(s[2], 1)), s),
)
LAUNCH = sorted(
    range(A),
    key=lambda a: ((0, 0.9, 1.8, 2.6, 4.4, 4.3, 3.6, 2.9)[a >> 2] + (0, 1.8, 5.0, 6.5)[a & 3], a),
)


def attn_at(a, shift, sign=1):
    return ((((a >> 2) + sign * shift[0]) & 7) << 2) | ((a + sign * shift[1]) & 3)


def ffn_at(f, shift):
    return ((((f >> 2) + shift[0]) & 3) << 2) | ((f & 3) ^ (2 * shift[1] + shift[2]))


def dot(a, b):
    return jnp.dot(a, b, preferred_element_type=F32)


def dot_nt(a, b):
    return lax.dot_general(a, b, (((1,), (1,)), ((), ())), preferred_element_type=F32)


def pair_of(f):
    return ((f >> 2) << 1) | (f & 1)


def in_pairs(x):
    return jnp.stack([x[(p >> 1) * 4 + z * 2 + (p & 1)] for p in range(F // 2) for z in range(2)], axis=0).reshape(
        (F // 2, 2) + x.shape[1:]
    )


def kernel(
    q_hbm, nk_hbm, nv_hbm, k_hbm, v_hbm, len_hbm, res_hbm, wo_hbm, gain_hbm, wg_hbm, wu_hbm, wd_hbm,
    fin,
    q_ref, nk_ref, nv_ref, len_ref, res_ref, gain_ref, k_s, v_s, wo_s, wg_s, wu_s, wd_s,
    snd_a, rcv_a, msg_b, rcv_b, snd_c, rcv_c, msg_e, rcv_e, snd_f, rcv_f, msg_g, rcv_g, snd_h, rcv_h,
    x_s, gath_s,
    load_sem, send_sem, recv_sem, recv_f_sem, give_send, give_recv, res_sem, res_s, near_sem, far_sem,
):
    a = lax.axis_index("attn")
    f = lax.axis_index("ffn")
    odd = (a >> 2) & 1
    gate_with = a ^ 4
    up_with = ((((a >> 2) + 2 * odd - 1) & 7) << 2) | (a & 3)
    owners = (a, gate_with, up_with)
    level = (f >> 1) & 1
    group = ((a >> 3) << 2) | (a & 3)

    core = f & 1
    sibling = (a, f ^ 1)
    barrier = pltpu.get_barrier_semaphore()

    def greet(peer):
        pl.semaphore_signal(barrier, inc=1, device_id=peer, device_id_type=MESH)

    for shift in FFN_SHIFTS:
        if shift[2] == 0:
            greet((a, ffn_at(f, shift) & ~1))

    @pl.when(core == 1)
    def _():
        greet(sibling)

    for shift in ATTN_SHIFTS:
        greet((attn_at(a, shift), f | 1))

    def load(src, dst, i):
        return pltpu.make_async_copy(src, dst, load_sem.at[i])

    small = [
        load(src, dst, 2 * ROWS + 6 + i)
        for i, (src, dst) in enumerate(
            [(q_hbm, q_ref), (nk_hbm, nk_ref), (nv_hbm, nv_ref), (len_hbm, len_ref), (res_hbm, res_ref), (gain_hbm, gain_ref.at[0])]
        )
    ]
    caches = [(load(k_hbm.at[r], k_s.at[r], 2 * r), load(v_hbm.at[r], v_s.at[r], 2 * r + 1)) for r in range(ROWS)]
    own_half = pl.ds(pl.multiple_of(odd * 4 * HD, HD), 3 * HD)
    their_half = pl.ds(pl.multiple_of((1 - odd) * 4 * HD, HD), 3 * HD)
    shared = pl.ds(3 * HD, HD)
    n0 = 2 * ROWS
    loads = [
        load(wo_hbm, wo_s, n0),
        load(wd_hbm, wd_s, n0 + 1),
        load(wg_hbm.at[:, own_half], wg_s.at[0, :, pl.ds(0, 3 * HD)], n0 + 2),
        load(wg_hbm.at[:, shared], wg_s.at[0, :, shared], n0 + 3),
        load(wu_hbm.at[:, own_half], wu_s.at[0, :, pl.ds(0, 3 * HD)], n0 + 4),
        load(wu_hbm.at[:, shared], wu_s.at[0, :, shared], n0 + 5),
    ]

    def give(src, dst, to, i):
        return pltpu.make_async_remote_copy(
            src_ref=src, dst_ref=dst, send_sem=give_send.at[i], recv_sem=give_recv.at[i],
            device_id=(to, f), device_id_type=MESH,
        )

    for copy in small:
        copy.start()
    for pair in caches:
        for copy in pair:
            copy.start()

    def to_ffn(src_of, dst, phase):
        for shift in FFN_SHIFTS:
            to = ffn_at(f, shift)
            pltpu.make_async_remote_copy(
                src_ref=src_of(to), dst_ref=dst.at[f], send_sem=send_sem.at[phase], recv_sem=recv_sem.at[phase],
                device_id=(a, to), device_id_type=MESH,
            ).start()

    def to_attn(src_of, dst, phase, sem_of):
        for shift in ATTN_SHIFTS:
            to = attn_at(a, shift)
            pltpu.make_async_remote_copy(
                src_ref=src_of(to), dst_ref=dst.at[a], send_sem=send_sem.at[phase], recv_sem=sem_of,
                device_id=(to, f), device_id_type=MESH,
            ).start()

    def wait_all(buf, n, sem):
        view = buf.at[pl.ds(0, n - 1)]
        pltpu.make_async_copy(view, view, sem).wait()

    lane = lax.broadcasted_iota(jnp.int32, (KV, HD), 1)
    col = lax.broadcasted_iota(jnp.int32, (KV, SPAN * KV), 1)
    kind, own_kind = col & 7, lane & 7
    place = (col >> 3) + f * SPAN
    own_ok = jnp.logical_and(lane < KV, jnp.full((KV, HD), f, jnp.int32) == 0)
    scale = 1.0 / math.sqrt(HD)
    pad = jnp.zeros((HD - KV, HD), BF)
    low_lane = lax.broadcasted_iota(jnp.int32, (HEADS, HD), 1) < HD // 2

    def fold(x, kinds):
        y = x[:KV]
        for k in range(1, KV):
            y = jnp.where(kinds == k, x[k * KV : (k + 1) * KV], y)
        return y

    def unfold(x, kinds):
        return jnp.concatenate([jnp.where(kinds == k, x, 0.0) for k in range(KV)], axis=0)

    def over_kinds(x, op):
        for turn in (8, 16, 32, 64):
            x = op(x, pltpu.roll(x, turn, 1))
        return x

    def spread(x):
        return jnp.concatenate([jnp.broadcast_to(x[:, k : k + 1], (KV, HD)) for k in range(KV)], axis=0)

    for copy in small:
        copy.wait()
    for k_copy, _ in caches:
        k_copy.wait()
    weights = []
    for r in range(ROWS):
        s = fold(dot_nt(q_ref[r], k_s[r]), kind) * scale
        s = jnp.where(place < len_ref[r], s, LOW)
        own = fold(dot_nt(q_ref[r], jnp.concatenate([nk_ref[r], pad], axis=0)), own_kind) * scale
        own = jnp.where(own_ok, own, LOW)
        m = own
        for t in range(KV):
            m = jnp.maximum(m, s[:, t * HD : (t + 1) * HD])
        m = jnp.maximum(over_kinds(m, jnp.maximum), FLOOR).astype(BF).astype(F32)
        p = [jnp.exp(s[:, t * HD : (t + 1) * HD] - m).astype(BF).astype(F32) for t in range(KV)]
        own_p = jnp.exp(own - m).astype(BF).astype(F32)
        total = own_p
        for t in range(KV):
            total = total + p[t]
        total = over_kinds(total, jnp.add)
        p = unfold(jnp.concatenate(p, axis=1), kind).astype(BF)
        weights.append((p, unfold(own_p, own_kind).astype(BF), jnp.where(low_lane, spread(m), spread(total))))
    for _, v_copy in caches:
        v_copy.wait()
    for r, (p, own_p, stats) in enumerate(weights):
        o = dot(p, v_s[r]) + dot(own_p, jnp.concatenate([nv_ref[r], pad], axis=0))
        x_s[pl.ds(r * HEADS, HEADS), :] = jnp.concatenate([o, stats], axis=1).astype(BF)
    for copy in loads:
        copy.start()
    n = ROWS * HEADS
    i = lax.broadcasted_iota(jnp.int32, (n, n), 0)
    j = lax.broadcasted_iota(jnp.int32, (n, n), 1)
    perm = (j == ((i >> 2) & 3) * HEADS + (i >> 4) * 4 + (i & 3)).astype(F32).astype(BF)
    snd_a[...] = dot(perm, x_s[...]).astype(BF).reshape(F, 16, 2 * HD)

    @pl.when(core == 0)
    def _():
        pl.semaphore_wait(barrier, F - 1)
        pl.semaphore_signal(near_sem, inc=1, device_id=sibling, device_id_type=MESH)

    @pl.when(core == 1)
    def _():
        pl.semaphore_wait(near_sem, 1)

    res = res_ref[...].astype(F32)
    res_s[level] = jnp.concatenate([res[:, :HD], res[:, HD:]], axis=0).astype(BF)
    to_ffn(lambda to: snd_a.at[to], rcv_a, 0)
    res_gift = pltpu.make_async_remote_copy(
        src_ref=res_s.at[level], dst_ref=res_s.at[level], send_sem=res_sem.at[0], recv_sem=res_sem.at[1],
        device_id=(a, f ^ 2), device_id_type=MESH,
    )
    res_gift.start()
    gifts = [
        give(wg_hbm.at[:, their_half], wg_s.at[1, :, pl.ds(0, 3 * HD)], gate_with, 0),
        give(wu_hbm.at[:, their_half], wu_s.at[1, :, pl.ds(0, 3 * HD)], up_with, 1),
        give(wg_hbm.at[:, shared], wg_s.at[1, :, shared], gate_with, 2),
        give(wu_hbm.at[:, shared], wu_s.at[1, :, shared], up_with, 3),
        give(gain_ref.at[0], gain_ref.at[1], gate_with, 4),
        give(gain_ref.at[0], gain_ref.at[2], up_with, 5),
    ]
    rcv_a[f] = snd_a[f]

    @pl.when(core == 1)
    def _():
        pl.semaphore_wait(barrier, 2 * (A - 1))
        pl.semaphore_signal(far_sem, inc=1, device_id=sibling, device_id_type=MESH)

    wait_all(rcv_a, F, recv_sem.at[0])

    parts = rcv_a[...].astype(F32)
    low3 = lax.broadcasted_iota(jnp.int32, (F, 16, HD), 2) < HD // 2
    stats = parts[:, :, HD:]
    turned = pltpu.roll(stats.reshape(F * 16, HD), HD // 2, 1).reshape(F, 16, HD)
    m = jnp.where(low3, stats, turned)
    t = jnp.where(low3, turned, stats)
    e = jnp.exp(m - jnp.max(m, axis=0, keepdims=True))
    att = jnp.sum(parts[:, :, :HD] * e, axis=0) / jnp.sum(t * e, axis=0)
    msg_b[...] = att.astype(BF)

    @pl.when(core == 0)
    def _():
        pl.semaphore_wait(far_sem, 1)

    to_attn(lambda to: msg_b, rcv_b, 1, recv_sem.at[1])
    for gift in gifts:
        gift.start()
    rcv_b[a] = msg_b[...]
    fin[:16] = msg_b[...].astype(F32)
    loads[0].wait()
    wait_all(rcv_b, A, recv_sem.at[1])

    gath_s[...] = rcv_b[...].astype(F32).reshape(A * 16, HD)
    lhs = jnp.concatenate([gath_s[pl.ds(h, A * ROWS, stride=4), :].astype(BF) for h in range(4)], axis=1)

    def halves(x):
        x = x.reshape(F, 8, 2 * HD)
        return jnp.concatenate([x[:, :, :HD], x[:, :, HD:]], axis=1)

    snd_c[...] = in_pairs(halves(dot(lhs, wo_s[...]))).astype(BF)
    for shift in FFN_SHIFTS:
        to = ffn_at(f, shift)
        pltpu.make_async_remote_copy(
            src_ref=snd_c.at[pair_of(to)], dst_ref=rcv_c.at[f], send_sem=send_sem.at[2], recv_sem=recv_sem.at[2],
            device_id=(a, to), device_id_type=MESH,
        ).start()
    rcv_c[f] = snd_c[pair_of(f)]
    res_gift.wait_recv()
    wait_all(rcv_c, F, recv_sem.at[2])
    msg_e[...] = (res_s[...].astype(F32) + jnp.sum(rcv_c[...].astype(F32), axis=0)).astype(BF)

    for x, c, w in BLOCK_SHIFTS:
        pltpu.make_async_remote_copy(
            src_ref=msg_e, dst_ref=rcv_e.at[w * (F // 2) + pair_of(f)], send_sem=send_sem.at[3], recv_sem=recv_sem.at[3],
            device_id=(owners[w], ffn_at(f, (x, 0, c))), device_id_type=MESH,
        ).start()
    rcv_e[pair_of(f)] = msg_e[...]
    for copy in loads[2:]:
        copy.wait()
    for gift in gifts:
        gift.wait_recv()
    wait_all(rcv_e, 3 * F // 2, recv_sem.at[3])
    wide = rcv_e[...].astype(F32).reshape(3, F, 16, HD)
    squares = jnp.zeros((F * 8, 1), F32)
    normed = []
    for w in range(3):
        left = wide[w, :, :8].reshape(F * 8, HD)
        right = wide[w, :, 8:].reshape(F * 8, HD)
        if w < 2:
            squares = squares + jnp.sum(left * left + right * right, axis=1, keepdims=True)
        gain = gain_ref[w]
        normed.append(jnp.concatenate([left * gain[:, :HD], right * gain[:, HD:]], axis=1).astype(BF))
    squares = jnp.broadcast_to(squares, (F * 8, HD))

    gate = dot(normed[0], wg_s[0]) + dot(normed[1], wg_s[1])
    up = dot(normed[0], wu_s[0]) + dot(normed[2], wu_s[1])
    low = lax.broadcasted_iota(jnp.int32, (F * 8, HD), 1) < HD // 2
    is_odd = jnp.full((F * 8, HD), odd, jnp.int32) == 1
    gate3, up3 = gate[:, 3 * HD :], up[:, 3 * HD :]
    gate3 = jnp.where(is_odd, pltpu.roll(gate3, HD // 2, 1), gate3)
    up3 = jnp.where(is_odd, up3, pltpu.roll(up3, HD // 2, 1))
    tiles = [gate[:, k * HD : (k + 1) * HD] for k in range(3)] + [jnp.where(low, gate3, up3)]
    tiles += [up[:, k * HD : (k + 1) * HD] for k in range(3)] + [squares]
    snd_f[...] = jnp.concatenate([t.reshape(F, 8, HD) for t in tiles], axis=1).astype(BF)
    for shift in COLUMN_SHIFTS:
        to = attn_at(a, shift)
        pltpu.make_async_remote_copy(
            src_ref=snd_f.at[((to >> 3) << 2) | (to & 3)], dst_ref=rcv_f.at[group], send_sem=send_sem.at[4],
            recv_sem=recv_f_sem.at[group], device_id=(to, f), device_id_type=MESH,
        ).start()
    acc = snd_f[group].astype(F32)
    for shift in reversed(COLUMN_SHIFTS):
        src = attn_at(a, shift, -1)
        src = ((src >> 3) << 2) | (src & 3)
        pltpu.make_async_copy(rcv_f.at[src], rcv_f.at[src], recv_f_sem.at[src]).wait()
        acc = acc + rcv_f[src].astype(F32)
    norm = lax.rsqrt(acc[56:] / D + 1e-5)
    norm = jnp.concatenate([norm] * 4, axis=0)
    gate = acc[:32] * norm
    half = pltpu.roll(gate[24:], HD // 2, 1)
    up = jnp.concatenate([acc[32:56] * norm[:24], half], axis=0)
    hidden = gate / (1.0 + jnp.exp(-gate)) * up
    low = lax.broadcasted_iota(jnp.int32, (8, HD), 1) < HD // 2
    is_odd = jnp.full((8, HD), odd, jnp.int32) == 1
    half = jnp.where(is_odd, pltpu.roll(hidden[24:], HD // 2, 1), hidden[24:])
    msg_g[...] = jnp.concatenate([hidden[:24], half], axis=0).astype(BF)

    for to in LAUNCH:

        @pl.when(a != to)
        def _():
            pltpu.make_async_remote_copy(
                src_ref=msg_g, dst_ref=rcv_g.at[a], send_sem=send_sem.at[5], recv_sem=recv_sem.at[5],
                device_id=(to, f), device_id_type=MESH,
            ).start()

    rcv_g[a] = msg_g[...]
    loads[1].wait()
    wait_all(rcv_g, A, recv_sem.at[5])
    hid = rcv_g[...].reshape(4, 2, 4, 32, HD).astype(F32)
    even = hid[:, 0].reshape(F, 32, HD)
    odds = hid[:, 1].reshape(F, 32, HD)
    low = lax.broadcasted_iota(jnp.int32, (F, 8, HD), 2) < HD // 2
    mid = jnp.where(low, even[:, 24:], odds[:, 24:])
    cols = [even[:, :8], even[:, 8:16], even[:, 16:24], mid, odds[:, :8], odds[:, 8:16], odds[:, 16:24]]
    hidden = jnp.concatenate([c.reshape(F * 8, HD) for c in cols], axis=1).astype(BF)
    snd_h[...] = halves(dot(hidden, wd_s[...])).astype(BF)
    to_ffn(lambda to: snd_h.at[pair_of(to) * 2 + ((to >> 1) & 1)], rcv_h, 6)
    rcv_h[f] = snd_h[pair_of(f) * 2 + level]
    wait_all(rcv_h, F, recv_sem.at[6])
    done = msg_e[level].astype(F32) + jnp.sum(rcv_h[...].astype(F32), axis=0)
    fin[16:] = done

    wait_all(rcv_a, F, send_sem.at[0])
    wait_all(rcv_b, A, send_sem.at[1])
    wait_all(rcv_c, F, send_sem.at[2])
    wait_all(rcv_e, 3 * F // 2, send_sem.at[3])
    res_gift.wait_send()
    wait_all(rcv_f, F, send_sem.at[4])
    wait_all(rcv_g, A, send_sem.at[5])
    wait_all(rcv_h, F, send_sem.at[6])
    for gift in gifts:
        gift.wait_send()


def finish(fin, att_out, layer_out):
    for h in range(4):
        att_out[:, h * HD : (h + 1) * HD] = fin[pl.ds(h, ROWS, stride=4), :].astype(BF)
    layer_out[...] = jnp.concatenate([fin[16:24], fin[24:]], axis=1).astype(BF)


def on_device(q, nk, nv, ck, cv, lengths, res, wo, gain, wg, wu, wd):
    vmem = pl.BlockSpec(memory_space=pltpu.VMEM)
    hbm = pl.BlockSpec(memory_space=pl.ANY)
    V = pltpu.VMEM
    fin = pl.pallas_call(
        kernel,
        out_shape=jax.ShapeDtypeStruct((32, HD), F32),
        in_specs=[hbm] * 12,
        out_specs=vmem,
        scratch_shapes=[
            V(q.shape, BF),
            V(nk.shape, BF),
            V(nv.shape, BF),
            pltpu.SMEM((ROWS,), jnp.int32),
            V(res.shape, BF),
            V((3, 1, 2 * HD), F32),
            V((ROWS, SPAN * KV, HD), BF),
            V((ROWS, SPAN * KV, HD), BF),
            V(wo.shape, BF),
            V((2, 2 * HD, 4 * HD), BF),
            V((2, 2 * HD, 4 * HD), BF),
            V(wd.shape, BF),
            V((F, 16, 2 * HD), BF),
            V((F, 16, 2 * HD), BF),
            V((16, HD), BF),
            V((A, 16, HD), BF),
            V((F // 2, 2, 16, HD), BF),
            V((F, 2, 16, HD), BF),
            V((2, 16, HD), BF),
            V((3 * F // 2, 2, 16, HD), BF),
            V((F, 64, HD), BF),
            V((F, 64, HD), BF),
            V((32, HD), BF),
            V((A, 32, HD), BF),
            V((F, 16, HD), BF),
            V((F, 16, HD), BF),
            V((ROWS * HEADS, 2 * HD), BF),
            V((A * 16, HD), F32),
            pltpu.SemaphoreType.DMA((2 * ROWS + 12,)),
            pltpu.SemaphoreType.DMA((7,)),
            pltpu.SemaphoreType.DMA((7,)),
            pltpu.SemaphoreType.DMA((F,)),
            pltpu.SemaphoreType.DMA((6,)),
            pltpu.SemaphoreType.DMA((6,)),
            pltpu.SemaphoreType.DMA((2,)),
            V((2, 16, HD), BF),
            pltpu.SemaphoreType.REGULAR,
            pltpu.SemaphoreType.REGULAR,
        ],
        compiler_params=pltpu.CompilerParams(
            collective_id=0, has_side_effects=True, vmem_limit_bytes=60 * 1024 * 1024
        ),
    )(
        q, nk, nv,
        ck.reshape(ROWS, SPAN * KV, HD), cv.reshape(ROWS, SPAN * KV, HD),
        lengths, res, wo, gain.reshape(1, 2 * HD), wg, wu, wd,
    )
    return pl.pallas_call(
        finish,
        out_shape=(jax.ShapeDtypeStruct((ROWS, 4 * HD), BF), jax.ShapeDtypeStruct((8, 2 * HD), BF)),
        in_specs=[vmem],
        out_specs=(vmem, vmem),
    )(fin)


def solution(mesh):
    in_specs = (
        P("attn", None, None),
        P("attn", None, None),
        P("attn", None, None),
        P("attn", "ffn", None, None),
        P("attn", "ffn", None, None),
        P("attn"),
        P("ffn", "attn"),
        P("ffn", "attn"),
        P("attn"),
        P("attn", "ffn"),
        P("attn", "ffn"),
        P("ffn", "attn"),
    )
    return jax.shard_map(
        on_device, mesh=mesh, in_specs=in_specs, out_specs=(P("attn", "ffn"), P("ffn", "attn")), check_vma=False
    )
```

```python
import functools
import math

import jax
import jax.numpy as jnp
from jax import lax
from jax.experimental import pallas as pl
from jax.experimental.pallas import tpu as pltpu
from jax.sharding import PartitionSpec as P

MESH = pl.DeviceIdType.MESH
D = 8192
A = 32
F = 16
ROWS = 4
HEADS = 64
KV = 8
HD = 128
SPAN = 128
LOW = -1e30
FLOOR = -1e29
BF = jnp.bfloat16
F32 = jnp.float32
ATTN_SHIFTS = sorted(
    ((y, z) for y in range(8) for z in range(4) if y or z),
    key=lambda s: (-(min(s[0], 8 - s[0]) + 2 * min(s[1], 4 - s[1])), s),
)
FFN_SHIFTS = sorted(
    ((x, z, c) for x in range(4) for z in range(2) for c in range(2) if x or z or c),
    key=lambda s: (-(min(s[0], 4 - s[0]) + s[1] + s[2] / 2), s),
)
COLUMN_SHIFTS = [s for s in ATTN_SHIFTS if s[0] % 2 == 0]
BLOCK_SHIFTS = sorted(
    ((x, c, w) for x in range(4) for c in range(2) for w in range(3) if x or c or w),
    key=lambda s: (-(min(s[0], 4 - s[0]) + s[1] / 2 + min(s[2], 1)), s),
)
LAUNCH = sorted(
    range(A),
    key=lambda a: ((0, 0.9, 1.8, 2.6, 4.4, 4.3, 3.6, 2.9)[a >> 2] + (0, 1.8, 5.0, 6.5)[a & 3], a),
)


def attn_at(a, shift, sign=1):
    return ((((a >> 2) + sign * shift[0]) & 7) << 2) | ((a + sign * shift[1]) & 3)


def ffn_at(f, shift):
    return ((((f >> 2) + shift[0]) & 3) << 2) | ((f & 3) ^ (2 * shift[1] + shift[2]))


def dot(a, b):
    return jnp.dot(a, b, preferred_element_type=F32)


def dot_nt(a, b):
    return lax.dot_general(a, b, (((1,), (1,)), ((), ())), preferred_element_type=F32)


def pair_of(f):
    return ((f >> 2) << 1) | (f & 1)


def in_pairs(x):
    return jnp.stack([x[(p >> 1) * 4 + z * 2 + (p & 1)] for p in range(F // 2) for z in range(2)], axis=0).reshape(
        (F // 2, 2) + x.shape[1:]
    )


def kernel(
    q_hbm, nk_hbm, nv_hbm, k_hbm, v_hbm, len_hbm, res_hbm, wo_hbm, gain_hbm, wg_hbm, wu_hbm, wd_hbm,
    fin_hbm,
    q_ref, nk_ref, nv_ref, len_ref, res_ref, gain_ref, k_s, v_s, wo_s, wg_s, wu_s, wd_s,
    snd_a, rcv_a, msg_b, rcv_b, snd_c, rcv_c, msg_e, rcv_e, snd_f, rcv_f, msg_g, rcv_g, snd_h, rcv_h,
    x_s, gath_s,
    load_sem, send_sem, recv_sem, recv_f_sem, give_send, give_recv, res_sem, res_s, near_sem, far_sem, fin, fin_sem,
):
    a = lax.axis_index("attn")
    f = lax.axis_index("ffn")
    odd = (a >> 2) & 1
    gate_with = a ^ 4
    up_with = ((((a >> 2) + 2 * odd - 1) & 7) << 2) | (a & 3)
    owners = (a, gate_with, up_with)
    level = (f >> 1) & 1
    group = ((a >> 3) << 2) | (a & 3)

    core = f & 1
    sibling = (a, f ^ 1)
    barrier = pltpu.get_barrier_semaphore()

    def greet(peer):
        pl.semaphore_signal(barrier, inc=1, device_id=peer, device_id_type=MESH)

    for shift in FFN_SHIFTS:
        if shift[2] == 0:
            greet((a, ffn_at(f, shift) & ~1))

    @pl.when(core == 1)
    def _():
        greet(sibling)

    for shift in ATTN_SHIFTS:
        greet((attn_at(a, shift), f | 1))

    def load(src, dst, i):
        return pltpu.make_async_copy(src, dst, load_sem.at[i])

    small = [
        load(src, dst, 2 * ROWS + 6 + i)
        for i, (src, dst) in enumerate(
            [(q_hbm, q_ref), (nk_hbm, nk_ref), (nv_hbm, nv_ref), (len_hbm, len_ref), (res_hbm, res_ref), (gain_hbm, gain_ref.at[0])]
        )
    ]
    caches = [(load(k_hbm.at[r], k_s.at[r], 2 * r), load(v_hbm.at[r], v_s.at[r], 2 * r + 1)) for r in range(ROWS)]
    own_half = pl.ds(pl.multiple_of(odd * 4 * HD, HD), 3 * HD)
    their_half = pl.ds(pl.multiple_of((1 - odd) * 4 * HD, HD), 3 * HD)
    shared = pl.ds(3 * HD, HD)
    n0 = 2 * ROWS
    loads = [
        load(wo_hbm, wo_s, n0),
        load(wd_hbm, wd_s, n0 + 1),
        load(wg_hbm.at[:, own_half], wg_s.at[0, :, pl.ds(0, 3 * HD)], n0 + 2),
        load(wg_hbm.at[:, shared], wg_s.at[0, :, shared], n0 + 3),
        load(wu_hbm.at[:, own_half], wu_s.at[0, :, pl.ds(0, 3 * HD)], n0 + 4),
        load(wu_hbm.at[:, shared], wu_s.at[0, :, shared], n0 + 5),
    ]

    def give(src, dst, to, i):
        return pltpu.make_async_remote_copy(
            src_ref=src, dst_ref=dst, send_sem=give_send.at[i], recv_sem=give_recv.at[i],
            device_id=(to, f), device_id_type=MESH,
        )

    for copy in small:
        copy.start()
    for pair in caches:
        for copy in pair:
            copy.start()

    def to_ffn(src_of, dst, phase):
        for shift in FFN_SHIFTS:
            to = ffn_at(f, shift)
            pltpu.make_async_remote_copy(
                src_ref=src_of(to), dst_ref=dst.at[f], send_sem=send_sem.at[phase], recv_sem=recv_sem.at[phase],
                device_id=(a, to), device_id_type=MESH,
            ).start()

    def to_attn(src_of, dst, phase, sem_of):
        for shift in ATTN_SHIFTS:
            to = attn_at(a, shift)
            pltpu.make_async_remote_copy(
                src_ref=src_of(to), dst_ref=dst.at[a], send_sem=send_sem.at[phase], recv_sem=sem_of,
                device_id=(to, f), device_id_type=MESH,
            ).start()

    def wait_all(buf, n, sem):
        view = buf.at[pl.ds(0, n - 1)]
        pltpu.make_async_copy(view, view, sem).wait()

    lane = lax.broadcasted_iota(jnp.int32, (KV, HD), 1)
    col = lax.broadcasted_iota(jnp.int32, (KV, SPAN * KV), 1)
    kind, own_kind = col & 7, lane & 7
    place = (col >> 3) + f * SPAN
    own_ok = jnp.logical_and(lane < KV, jnp.full((KV, HD), f, jnp.int32) == 0)
    scale = 1.0 / math.sqrt(HD)
    pad = jnp.zeros((HD - KV, HD), BF)
    low_lane = lax.broadcasted_iota(jnp.int32, (HEADS, HD), 1) < HD // 2

    def fold(x, kinds):
        y = x[:KV]
        for k in range(1, KV):
            y = jnp.where(kinds == k, x[k * KV : (k + 1) * KV], y)
        return y

    def unfold(x, kinds):
        return jnp.concatenate([jnp.where(kinds == k, x, 0.0) for k in range(KV)], axis=0)

    def over_kinds(x, op):
        for turn in (8, 16, 32, 64):
            x = op(x, pltpu.roll(x, turn, 1))
        return x

    def spread(x):
        return jnp.concatenate([jnp.broadcast_to(x[:, k : k + 1], (KV, HD)) for k in range(KV)], axis=0)

    for copy in small:
        copy.wait()
    for k_copy, _ in caches:
        k_copy.wait()
    weights = []
    for r in range(ROWS):
        s = fold(dot_nt(q_ref[r], k_s[r]), kind) * scale
        s = jnp.where(place < len_ref[r], s, LOW)
        own = fold(dot_nt(q_ref[r], jnp.concatenate([nk_ref[r], pad], axis=0)), own_kind) * scale
        own = jnp.where(own_ok, own, LOW)
        m = own
        for t in range(KV):
            m = jnp.maximum(m, s[:, t * HD : (t + 1) * HD])
        m = jnp.maximum(over_kinds(m, jnp.maximum), FLOOR).astype(BF).astype(F32)
        p = [jnp.exp(s[:, t * HD : (t + 1) * HD] - m).astype(BF).astype(F32) for t in range(KV)]
        own_p = jnp.exp(own - m).astype(BF).astype(F32)
        total = own_p
        for t in range(KV):
            total = total + p[t]
        total = over_kinds(total, jnp.add)
        p = unfold(jnp.concatenate(p, axis=1), kind).astype(BF)
        weights.append((p, unfold(own_p, own_kind).astype(BF), jnp.where(low_lane, spread(m), spread(total))))
    for _, v_copy in caches:
        v_copy.wait()
    for r, (p, own_p, stats) in enumerate(weights):
        o = dot(p, v_s[r]) + dot(own_p, jnp.concatenate([nv_ref[r], pad], axis=0))
        x_s[pl.ds(r * HEADS, HEADS), :] = jnp.concatenate([o, stats], axis=1).astype(BF)
    for copy in loads:
        copy.start()
    n = ROWS * HEADS
    i = lax.broadcasted_iota(jnp.int32, (n, n), 0)
    j = lax.broadcasted_iota(jnp.int32, (n, n), 1)
    perm = (j == ((i >> 2) & 3) * HEADS + (i >> 4) * 4 + (i & 3)).astype(F32).astype(BF)
    snd_a[...] = dot(perm, x_s[...]).astype(BF).reshape(F, 16, 2 * HD)

    @pl.when(core == 0)
    def _():
        pl.semaphore_wait(barrier, F - 1)
        pl.semaphore_signal(near_sem, inc=1, device_id=sibling, device_id_type=MESH)

    @pl.when(core == 1)
    def _():
        pl.semaphore_wait(near_sem, 1)

    res = res_ref[...].astype(F32)
    res_s[level] = jnp.concatenate([res[:, :HD], res[:, HD:]], axis=0).astype(BF)
    to_ffn(lambda to: snd_a.at[to], rcv_a, 0)
    res_gift = pltpu.make_async_remote_copy(
        src_ref=res_s.at[level], dst_ref=res_s.at[level], send_sem=res_sem.at[0], recv_sem=res_sem.at[1],
        device_id=(a, f ^ 2), device_id_type=MESH,
    )
    res_gift.start()
    gifts = [
        give(wg_hbm.at[:, their_half], wg_s.at[1, :, pl.ds(0, 3 * HD)], gate_with, 0),
        give(wu_hbm.at[:, their_half], wu_s.at[1, :, pl.ds(0, 3 * HD)], up_with, 1),
        give(wg_hbm.at[:, shared], wg_s.at[1, :, shared], gate_with, 2),
        give(wu_hbm.at[:, shared], wu_s.at[1, :, shared], up_with, 3),
        give(gain_ref.at[0], gain_ref.at[1], gate_with, 4),
        give(gain_ref.at[0], gain_ref.at[2], up_with, 5),
    ]
    rcv_a[f] = snd_a[f]

    @pl.when(core == 1)
    def _():
        pl.semaphore_wait(barrier, 2 * (A - 1))
        pl.semaphore_signal(far_sem, inc=1, device_id=sibling, device_id_type=MESH)

    wait_all(rcv_a, F, recv_sem.at[0])

    parts = rcv_a[...].astype(F32)
    low3 = lax.broadcasted_iota(jnp.int32, (F, 16, HD), 2) < HD // 2
    stats = parts[:, :, HD:]
    turned = pltpu.roll(stats.reshape(F * 16, HD), HD // 2, 1).reshape(F, 16, HD)
    m = jnp.where(low3, stats, turned)
    t = jnp.where(low3, turned, stats)
    e = jnp.exp(m - jnp.max(m, axis=0, keepdims=True))
    att = jnp.sum(parts[:, :, :HD] * e, axis=0) / jnp.sum(t * e, axis=0)
    msg_b[...] = att.astype(BF)

    @pl.when(core == 0)
    def _():
        pl.semaphore_wait(far_sem, 1)

    to_attn(lambda to: msg_b, rcv_b, 1, recv_sem.at[1])
    for gift in gifts:
        gift.start()
    rcv_b[a] = msg_b[...]
    fin[:16] = msg_b[...].astype(F32)
    loads[0].wait()
    wait_all(rcv_b, A, recv_sem.at[1])

    gath_s[...] = rcv_b[...].astype(F32).reshape(A * 16, HD)
    lhs = jnp.concatenate([gath_s[pl.ds(h, A * ROWS, stride=4), :].astype(BF) for h in range(4)], axis=1)

    def halves(x):
        x = x.reshape(F, 8, 2 * HD)
        return jnp.concatenate([x[:, :, :HD], x[:, :, HD:]], axis=1)

    snd_c[...] = in_pairs(halves(dot(lhs, wo_s[...]))).astype(BF)
    for shift in FFN_SHIFTS:
        to = ffn_at(f, shift)
        pltpu.make_async_remote_copy(
            src_ref=snd_c.at[pair_of(to)], dst_ref=rcv_c.at[f], send_sem=send_sem.at[2], recv_sem=recv_sem.at[2],
            device_id=(a, to), device_id_type=MESH,
        ).start()
    rcv_c[f] = snd_c[pair_of(f)]
    res_gift.wait_recv()
    wait_all(rcv_c, F, recv_sem.at[2])
    msg_e[...] = (res_s[...].astype(F32) + jnp.sum(rcv_c[...].astype(F32), axis=0)).astype(BF)

    for x, c, w in BLOCK_SHIFTS:
        pltpu.make_async_remote_copy(
            src_ref=msg_e, dst_ref=rcv_e.at[w * (F // 2) + pair_of(f)], send_sem=send_sem.at[3], recv_sem=recv_sem.at[3],
            device_id=(owners[w], ffn_at(f, (x, 0, c))), device_id_type=MESH,
        ).start()
    rcv_e[pair_of(f)] = msg_e[...]
    for copy in loads[2:]:
        copy.wait()
    for gift in gifts:
        gift.wait_recv()
    wait_all(rcv_e, 3 * F // 2, recv_sem.at[3])
    wide = rcv_e[...].astype(F32).reshape(3, F, 16, HD)
    squares = jnp.zeros((F * 8, 1), F32)
    normed = []
    for w in range(3):
        left = wide[w, :, :8].reshape(F * 8, HD)
        right = wide[w, :, 8:].reshape(F * 8, HD)
        if w < 2:
            squares = squares + jnp.sum(left * left + right * right, axis=1, keepdims=True)
        gain = gain_ref[w]
        normed.append(jnp.concatenate([left * gain[:, :HD], right * gain[:, HD:]], axis=1).astype(BF))
    squares = jnp.broadcast_to(squares, (F * 8, HD))

    gate = dot(normed[0], wg_s[0]) + dot(normed[1], wg_s[1])
    up = dot(normed[0], wu_s[0]) + dot(normed[2], wu_s[1])
    low = lax.broadcasted_iota(jnp.int32, (F * 8, HD), 1) < HD // 2
    is_odd = jnp.full((F * 8, HD), odd, jnp.int32) == 1
    gate3, up3 = gate[:, 3 * HD :], up[:, 3 * HD :]
    gate3 = jnp.where(is_odd, pltpu.roll(gate3, HD // 2, 1), gate3)
    up3 = jnp.where(is_odd, up3, pltpu.roll(up3, HD // 2, 1))
    tiles = [gate[:, k * HD : (k + 1) * HD] for k in range(3)] + [jnp.where(low, gate3, up3)]
    tiles += [up[:, k * HD : (k + 1) * HD] for k in range(3)] + [squares]
    snd_f[...] = jnp.concatenate([t.reshape(F, 8, HD) for t in tiles], axis=1).astype(BF)
    for shift in COLUMN_SHIFTS:
        to = attn_at(a, shift)
        pltpu.make_async_remote_copy(
            src_ref=snd_f.at[((to >> 3) << 2) | (to & 3)], dst_ref=rcv_f.at[group], send_sem=send_sem.at[4],
            recv_sem=recv_f_sem.at[group], device_id=(to, f), device_id_type=MESH,
        ).start()
    acc = snd_f[group].astype(F32)
    for shift in reversed(COLUMN_SHIFTS):
        src = attn_at(a, shift, -1)
        src = ((src >> 3) << 2) | (src & 3)
        pltpu.make_async_copy(rcv_f.at[src], rcv_f.at[src], recv_f_sem.at[src]).wait()
        acc = acc + rcv_f[src].astype(F32)
    norm = lax.rsqrt(acc[56:] / D + 1e-5)
    norm = jnp.concatenate([norm] * 4, axis=0)
    gate = acc[:32] * norm
    half = pltpu.roll(gate[24:], HD // 2, 1)
    up = jnp.concatenate([acc[32:56] * norm[:24], half], axis=0)
    hidden = gate / (1.0 + jnp.exp(-gate)) * up
    low = lax.broadcasted_iota(jnp.int32, (8, HD), 1) < HD // 2
    is_odd = jnp.full((8, HD), odd, jnp.int32) == 1
    half = jnp.where(is_odd, pltpu.roll(hidden[24:], HD // 2, 1), hidden[24:])
    msg_g[...] = jnp.concatenate([hidden[:24], half], axis=0).astype(BF)

    for to in LAUNCH:

        @pl.when(a != to)
        def _():
            pltpu.make_async_remote_copy(
                src_ref=msg_g, dst_ref=rcv_g.at[a], send_sem=send_sem.at[5], recv_sem=recv_sem.at[5],
                device_id=(to, f), device_id_type=MESH,
            ).start()

    rcv_g[a] = msg_g[...]
    loads[1].wait()
    wait_all(rcv_g, A, recv_sem.at[5])
    hid = rcv_g[...].reshape(4, 2, 4, 32, HD).astype(F32)
    even = hid[:, 0].reshape(F, 32, HD)
    odds = hid[:, 1].reshape(F, 32, HD)
    low = lax.broadcasted_iota(jnp.int32, (F, 8, HD), 2) < HD // 2
    mid = jnp.where(low, even[:, 24:], odds[:, 24:])
    cols = [even[:, :8], even[:, 8:16], even[:, 16:24], mid, odds[:, :8], odds[:, 8:16], odds[:, 16:24]]
    hidden = jnp.concatenate([c.reshape(F * 8, HD) for c in cols], axis=1).astype(BF)
    snd_h[...] = halves(dot(hidden, wd_s[...])).astype(BF)
    to_ffn(lambda to: snd_h.at[pair_of(to) * 2 + ((to >> 1) & 1)], rcv_h, 6)
    rcv_h[f] = snd_h[pair_of(f) * 2 + level]
    wait_all(rcv_h, F, recv_sem.at[6])
    done = msg_e[level].astype(F32) + jnp.sum(rcv_h[...].astype(F32), axis=0)
    fin[16:] = done

    result = pltpu.make_async_copy(fin, fin_hbm, fin_sem)
    result.start()

    wait_all(rcv_a, F, send_sem.at[0])
    wait_all(rcv_b, A, send_sem.at[1])
    wait_all(rcv_c, F, send_sem.at[2])
    wait_all(rcv_e, 3 * F // 2, send_sem.at[3])
    res_gift.wait_send()
    wait_all(rcv_f, F, send_sem.at[4])
    wait_all(rcv_g, A, send_sem.at[5])
    wait_all(rcv_h, F, send_sem.at[6])
    for gift in gifts:
        gift.wait_send()
    result.wait()


def finish(fin, att_out, layer_out):
    for h in range(4):
        att_out[:, h * HD : (h + 1) * HD] = fin[pl.ds(h, ROWS, stride=4), :].astype(BF)
    layer_out[...] = jnp.concatenate([fin[16:24], fin[24:]], axis=1).astype(BF)


def on_device(q, nk, nv, ck, cv, lengths, res, wo, gain, wg, wu, wd):
    vmem = pl.BlockSpec(memory_space=pltpu.VMEM)
    hbm = pl.BlockSpec(memory_space=pl.ANY)
    V = pltpu.VMEM
    fin = pl.pallas_call(
        kernel,
        out_shape=jax.ShapeDtypeStruct((32, HD), F32),
        in_specs=[hbm] * 12,
        out_specs=hbm,
        scratch_shapes=[
            V(q.shape, BF),
            V(nk.shape, BF),
            V(nv.shape, BF),
            pltpu.SMEM((ROWS,), jnp.int32),
            V(res.shape, BF),
            V((3, 1, 2 * HD), F32),
            V((ROWS, SPAN * KV, HD), BF),
            V((ROWS, SPAN * KV, HD), BF),
            V(wo.shape, BF),
            V((2, 2 * HD, 4 * HD), BF),
            V((2, 2 * HD, 4 * HD), BF),
            V(wd.shape, BF),
            V((F, 16, 2 * HD), BF),
            V((F, 16, 2 * HD), BF),
            V((16, HD), BF),
            V((A, 16, HD), BF),
            V((F // 2, 2, 16, HD), BF),
            V((F, 2, 16, HD), BF),
            V((2, 16, HD), BF),
            V((3 * F // 2, 2, 16, HD), BF),
            V((F, 64, HD), BF),
            V((F, 64, HD), BF),
            V((32, HD), BF),
            V((A, 32, HD), BF),
            V((F, 16, HD), BF),
            V((F, 16, HD), BF),
            V((ROWS * HEADS, 2 * HD), BF),
            V((A * 16, HD), F32),
            pltpu.SemaphoreType.DMA((2 * ROWS + 12,)),
            pltpu.SemaphoreType.DMA((7,)),
            pltpu.SemaphoreType.DMA((7,)),
            pltpu.SemaphoreType.DMA((F,)),
            pltpu.SemaphoreType.DMA((6,)),
            pltpu.SemaphoreType.DMA((6,)),
            pltpu.SemaphoreType.DMA((2,)),
            V((2, 16, HD), BF),
            pltpu.SemaphoreType.REGULAR,
            pltpu.SemaphoreType.REGULAR,
            V((32, HD), F32),
            pltpu.SemaphoreType.DMA,
        ],
        compiler_params=pltpu.CompilerParams(
            collective_id=0, has_side_effects=True, vmem_limit_bytes=60 * 1024 * 1024
        ),
    )(
        q, nk, nv,
        ck.reshape(ROWS, SPAN * KV, HD), cv.reshape(ROWS, SPAN * KV, HD),
        lengths, res, wo, gain.reshape(1, 2 * HD), wg, wu, wd,
    )
    return pl.pallas_call(
        finish,
        out_shape=(jax.ShapeDtypeStruct((ROWS, 4 * HD), BF), jax.ShapeDtypeStruct((8, 2 * HD), BF)),
        in_specs=[vmem],
        out_specs=(vmem, vmem),
    )(fin)


def solution(mesh):
    in_specs = (
        P("attn", None, None),
        P("attn", None, None),
        P("attn", None, None),
        P("attn", "ffn", None, None),
        P("attn", "ffn", None, None),
        P("attn"),
        P("ffn", "attn"),
        P("ffn", "attn"),
        P("attn"),
        P("attn", "ffn"),
        P("attn", "ffn"),
        P("ffn", "attn"),
    )
    return jax.shard_map(
        on_device, mesh=mesh, in_specs=in_specs, out_specs=(P("attn", "ffn"), P("ffn", "attn")), check_vma=False
    )
```
